32 devices in a mesh: pole: 4 (over y, x), row: 4 (over z), col: 2 (over core).
Axes of the slice: x: 2, y: 2, z: 4, core: 2. Of those that a mesh axis runs over, the one named last changes fastest.
Arguments:
- root_inverse: float32 [8, 1024, 1024], P('pole', ('row', 'col')), may hold values from -100 to 100
- node_factor: float32 [8, 4, 1024, 512], P('pole', 'row', None, 'col'), may hold values from -0.1875 to 0.1875
- node_inverse: float32 [8, 4, 512, 512], P('pole', 'row'), may hold values from -100 to 100
- leaf_root_factor: float32 [8, 8, 1024, 256], P('pole', ('row', 'col')), may hold values from -0.1875 to 0.1875
- leaf_node_factor: float32 [8, 8, 512, 256], P('pole', ('row', 'col')), may hold values from -0.25 to 0.25
- leaf_inverse: float32 [8, 8, 256, 256], P('pole', ('row', 'col')), may hold values from -100 to 100
- leaf_pattern: int32 [8, 8], P(('row', 'col')), may hold values 0 or 1
- pole_weight: float32 [8], P('pole'), may hold values from 0.1 to 1
Outputs:
- root_block: float32 [1024, 1024], P(('row', 'col'))
- node_offdiag: float32 [4, 1024, 512], P('row', None, 'col')
- node_diag: float32 [4, 512, 512], P('row', 'col')
- leaf_root: float32 [8, 1024, 256], P(('row', 'col'))
- leaf_node: float32 [8, 512, 256], P(('row', 'col'))
- leaf_diag: float32 [8, 256, 256], P(('row', 'col'))
The draws below stay inside these ranges and needn't reach their ends.
All inputs are finite; a program needn't handle non-finite values. No bound on the sum of `leaf_pattern` on one device may be relied on, other than what follows from the above.
Results may differ from the reference program's by a relative error of at most 0.0001.
Values sent between devices are 32-bit elements; how exact they have to be, the bound alone decides.
No kernel may reach another device: no remote copies, remote signals or barrier semaphores. Data moves between devices by JAX's collectives and lax.ppermute only.
A program may use at most 64 MiB of HBM per device.

```python
import math
import jax
import jax.numpy as jnp
from jax import lax

W0 = 1024
W1 = 512
W2 = 256
BLOCK = 128
POLES = 8
N1 = 4
NLEAF = 8
RB = 8
N_COL = 2


def draw_diagonal_block(key, lead_shape, order):
    first_key, second_key = jax.random.split(key, 2)
    normal_part = jnp.clip(jax.random.normal(first_key, lead_shape + (order, order), jnp.float32), -6.0, 6.0)
    offdiag = normal_part * (1.0 / math.sqrt(order))
    diagonal = jax.random.uniform(second_key, lead_shape + (order,), jnp.float32, 0.5, 2.0)
    return offdiag + diagonal[..., None] * jnp.eye(order, dtype=jnp.float32)


def draw_root_inverse(key, part):
    return draw_diagonal_block(jax.random.fold_in(key, 11), (POLES,), W0)


def draw_node_inverse(key, part):
    return draw_diagonal_block(jax.random.fold_in(key, 12), (POLES, N1), W1)


def draw_leaf_inverse(key, part):
    return draw_diagonal_block(jax.random.fold_in(key, 13), (POLES, NLEAF), W2)


def plant(result, stream_key, least, high):
    dims = result.shape
    place = [jax.random.randint(jax.random.fold_in(stream_key, axis), (), 0, dims[axis]) for axis in range(len(dims))]
    result = result.at[tuple(place)].set(least)
    longest = dims.index(max(dims))
    place[longest] = (place[longest] + 1) % dims[longest]
    return result.at[tuple(place)].set(high)


def levels(own_key, extent, cuts, smallest, top_value):
    factor_of = 1.0
    for position, parts in cuts:
        steps = jax.random.uniform(jax.random.fold_in(jax.random.fold_in(own_key, 6), position), (parts,), jnp.float32, smallest / len(cuts), top_value / len(cuts))
        factor_of = factor_of * jnp.repeat(jnp.exp(steps), extent[position] // parts).reshape((-1,) + (1,) * (len(extent) - 1 - position))
    return factor_of


def bell_draw(stream_key, shape, deviation, most, shards=(), held_as=jnp.bfloat16):
    factor_of = levels(stream_key, shape, shards, -0.22, 0.18) if shards else 1.0
    drawn = jax.random.normal(stream_key, shape, jnp.float32) * deviation * factor_of
    return jnp.minimum(jnp.maximum(drawn, -most), most).astype(held_as)


def setup_inputs(seed: int = 0) -> dict:
    splits = jax.random.split(jax.random.key(seed), 9)
    return {
        "root_inverse": draw_root_inverse(jax.random.fold_in(splits[8], 71), 0),
        "node_factor": bell_draw(splits[1], (POLES, N1, W0, W1), W0 ** -0.5, 0.1875, ((0, 4), (1, 4), (3, 2)), jnp.float32),
        "node_inverse": draw_node_inverse(jax.random.fold_in(splits[8], 71), 0),
        "leaf_root_factor": bell_draw(splits[3], (POLES, NLEAF, W0, W2), W0 ** -0.5, 0.1875, ((0, 4), (1, 8)), jnp.float32),
        "leaf_node_factor": bell_draw(splits[4], (POLES, NLEAF, W1, W2), W1 ** -0.5, 0.25, ((0, 4), (1, 8)), jnp.float32),
        "leaf_inverse": draw_leaf_inverse(jax.random.fold_in(splits[8], 71), 0),
        "leaf_pattern": plant((jax.random.randint(splits[6], (NLEAF, RB), 0, 2) < 1).astype(jnp.int32), jax.random.fold_in(splits[6], 1), 0, 1),
        "pole_weight": jnp.clip(jnp.exp(math.log(1.0) - 2.3025851 * jax.random.uniform(splits[7], (POLES,), jnp.float32) ** levels(splits[7], (POLES,), ((0, 4),), -0.2, 0.2)), 0.1, 1.0),
    }


highest = lax.Precision.HIGHEST


def product(left, right):
    return jnp.matmul(left, right, precision=highest)


def reference(root_inverse, node_factor, node_inverse, leaf_root_factor, leaf_node_factor, leaf_inverse, leaf_pattern, pole_weight):
    row_mask = jnp.repeat(leaf_pattern.astype(jnp.float32), BLOCK, axis=1)
    parent = jnp.arange(NLEAF, dtype=jnp.int32) // N_COL
    totals = None
    for pole_index in range(POLES):
        weight = pole_weight[pole_index]
        root_now = root_inverse[pole_index]
        factor_now = node_factor[pole_index]
        offdiag = -product(root_now[None], factor_now)
        sepdiag = node_inverse[pole_index] - product(jnp.swapaxes(factor_now, 1, 2), offdiag)
        masked = leaf_root_factor[pole_index] * row_mask[:, :, None]
        node_leaf = leaf_node_factor[pole_index]
        parent_off = offdiag[parent]
        parent_diag = sepdiag[parent]
        upper = -(product(root_now[None], masked) + product(parent_off, node_leaf))
        middle = -(product(jnp.swapaxes(parent_off, 1, 2), masked) + product(parent_diag, node_leaf))
        lower = leaf_inverse[pole_index] - product(jnp.swapaxes(masked, 1, 2), upper) - product(jnp.swapaxes(node_leaf, 1, 2), middle)
        terms = (root_now, offdiag, sepdiag, upper, middle, lower)
        terms = tuple(weight * item for item in terms)
        if totals is None:
            totals = terms
        else:
            totals = tuple(first + second for first, second in zip(totals, terms))
    return (totals[0], totals[1], totals[2], totals[3], totals[4], totals[5])
```

```python
import functools

import jax
import jax.numpy as jnp
from jax import lax
from jax.experimental import pallas as pl
from jax.experimental.pallas import tpu as pltpu
from jax.sharding import PartitionSpec as P

HIGH = lax.Precision.HIGH
SWAP = [(0, 1), (1, 0)]
MIB = 1 << 20


def product(left, right):
    return jnp.matmul(left, right, precision=HIGH)


def left_t(left, right):
    return jnp.einsum("pki,pkj->pij", left, right, precision=HIGH)


def weighted(weights, values):
    return jnp.sum(weights[:, None, None] * values, axis=0)


def general(
    root_inverse,
    node_factor,
    node_inverse,
    leaf_root_factor,
    leaf_node_factor,
    leaf_inverse,
    leaf_pattern,
    pole_weight,
):
    inv_n, leaf_n, inv_l = node_inverse[:, 0], leaf_node_factor[:, 0], leaf_inverse[:, 0]
    w1, width = inv_n.shape[2], node_factor.shape[3]
    start = lax.axis_index("col") * width
    row_mask = jnp.repeat(leaf_pattern[0].astype(jnp.float32), leaf_root_factor.shape[2] // leaf_pattern.shape[1])
    leaf = leaf_root_factor[:, 0] * row_mask[None, :, None]
    factor = lax.all_gather(node_factor[:, 0], "col", axis=2, tiled=True)
    root = lax.all_gather(root_inverse, ("row", "col"), axis=1, tiled=True)
    x = product(root, jnp.concatenate([factor, leaf - product(factor, leaf_n)], axis=2))
    gram = left_t(jnp.concatenate([factor, leaf], axis=2), x)
    sep = inv_n + gram[:, :w1, :w1]
    middle = jnp.swapaxes(gram[:, w1:, :w1], 1, 2) - product(sep, leaf_n)
    lower = inv_l + gram[:, w1:, w1:] - left_t(leaf_n, middle)
    rows = -weighted(pole_weight, x)
    totals = lax.psum(
        (
            weighted(pole_weight, root_inverse),
            lax.dynamic_slice_in_dim(rows, start, width, 1),
            lax.dynamic_slice_in_dim(weighted(pole_weight, sep), start, width, 0),
            rows[:, w1:],
            weighted(pole_weight, middle),
            weighted(pole_weight, lower),
        ),
        "pole",
    )
    return (totals[0],) + tuple(t[None] for t in totals[1:])


def split(x):
    high = x.astype(jnp.bfloat16)
    return high, (x - high.astype(jnp.float32)).astype(jnp.bfloat16)


def dot3(left, right, dims=((1,), (0,))):
    def one(a, b):
        return lax.dot_general(a, b, (dims, ((), ())), preferred_element_type=jnp.float32)

    return one(left[0], right[0]) + (one(left[0], right[1]) + one(left[1], right[0]))


def prepare_kernel(block, where, pattern, f_own, f_other, leaf, leaf_n, w_high, w_low, l_high, l_low, n_high, n_low):
    first = where[0] == 0
    own, other = f_own[0], f_other[0]
    f = jnp.concatenate([jnp.where(first, own, other), jnp.where(first, other, own)], axis=1)
    rows, w1 = f.shape
    step = pl.program_id(1)
    masked = []
    for i in range(0, rows, block):
        keep = pattern[0, step * (rows // block) + i // block]
        masked.append(jnp.where(keep != 0, leaf[0, i : i + block], 0.0))
    masked = jnp.concatenate(masked, axis=0)

    @pl.when(step == 0)
    def _():
        n_high[...], n_low[...] = split(leaf_n[0])

    fs = split(f)
    ds = split(masked - dot3(fs, (n_high[...], n_low[...])))
    w_high[0, :, :w1], w_low[0, :, :w1] = fs
    w_high[0, :, w1:], w_low[0, :, w1:] = ds
    l_high[0], l_low[0] = split(masked)


def prepare(where, pattern, f_own, f_other, leaf, leaf_n):
    poles, w0, width = f_own.shape
    w1, w2 = leaf_n.shape[1:]
    rows = 256
    lanes = w1 + w2

    def spec(*tail):
        return pl.BlockSpec((1, rows) + tail, lambda p, i, w, t: (p, i, 0))

    def out(*tail):
        return jax.ShapeDtypeStruct((poles, w0) + tail, jnp.bfloat16)

    return pl.pallas_call(
        functools.partial(prepare_kernel, w0 // pattern.shape[1]),
        grid_spec=pltpu.PrefetchScalarGridSpec(
            num_scalar_prefetch=2,
            grid=(poles, w0 // rows),
            in_specs=[spec(width), spec(width), spec(w2), pl.BlockSpec((1, w1, w2), lambda p, i, w, t: (p, 0, 0))],
            out_specs=[spec(lanes), spec(lanes), spec(w2), spec(w2)],
            scratch_shapes=[pltpu.VMEM((w1, w2), jnp.bfloat16)] * 2,
        ),
        out_shape=[out(lanes), out(lanes), out(w2), out(w2)],
        compiler_params=pltpu.CompilerParams(vmem_limit_bytes=24 * MIB),
        cost_estimate=pl.CostEstimate(flops=6 * poles * w0 * w1 * w2, bytes_accessed=15 * MIB, transcendentals=0),
        name="prepare",
    )(where, pattern, f_own, f_other, leaf, leaf_n)


def unit_kernel(choices, first_unit, last, pieces, where, weight, *refs):
    shards, refs = refs[: 2 * choices], refs[2 * choices :]
    (w_high, w_low, l_high, l_low), refs = refs[:4], refs[4:]
    if not first_unit:
        (gram_in, square_in), refs = refs[:2], refs[2:]
    if last:
        (inv_n, leaf_n, inv_l), refs = refs[:3], refs[3:]
    outs, refs = refs[:pieces], refs[pieces:]
    if not last:
        (gram, square), refs = refs[:2], refs[2:]
    (r_high, r_low) = refs
    p = pl.program_id(0)
    col, owner = where[0], where[1]
    rows = shards[0].shape[1]
    unit = 2 * rows
    for i in range(2):
        value = shards[i][0]
        if choices == 2:
            value = jnp.where(where[2] == 0, value, shards[2 + i][0])
        at = pl.ds(pl.multiple_of(jnp.where(col == i, 0, rows), rows), rows)
        r_high[at], r_low[at] = split(value)
    lanes = w_high.shape[2]
    w2 = l_high.shape[2]
    w1 = lanes - w2
    width = w1 // 2
    x = dot3((r_high[...], r_low[...]), (w_high[0], w_low[0]))
    scale = weight[p]
    mine = jnp.where(col == 0, x[:, :width], x[:, width:w1])
    sent = -scale * jnp.concatenate([mine, x[:, w1:]], axis=1)
    here = pl.ds(pl.multiple_of(owner * unit, unit), unit)
    fs = (w_high[0, here, :w1], w_low[0, here, :w1])
    ls = (l_high[0, here], l_low[0, here])
    xs = split(x)
    ps = (xs[0][:, :w1], xs[1][:, :w1])
    us = (xs[0][:, w1:], xs[1][:, w1:])
    across = ((0,), (0,))
    cross = dot3(fs, ps, across)
    below = dot3(ls, ps, across)
    inner = dot3(ls, us, across)
    if not first_unit:
        cross = cross + gram_in[0, :w1]
        below = below + gram_in[0, w1:]
        inner = inner + square_in[0]

    def put(ref, at, value):
        @pl.when(p == 0)
        def _():
            ref[at] = value

        @pl.when(p > 0)
        def _():
            ref[at] += value

    if not last:
        gram[0, :w1] = cross
        gram[0, w1:] = below
        square[0] = inner
        if first_unit:
            put(outs[0], slice(None), sent)
            root = scale * shards[0][0]
            half = root.shape[1] // 2
            put(outs[1], slice(0, rows), root[:, :half])
            put(outs[1], slice(rows, 2 * rows), root[:, half:])
        else:
            put(outs[0], slice(None), sent[:rows])
            put(outs[1], slice(None), sent[rows:])
        return
    sep = inv_n[0] + cross
    ns = split(leaf_n[0])
    middle = below.T - dot3(split(sep), ns)
    lower = inv_l[0] + inner - dot3(ns, split(middle), across)
    sep = scale * jnp.where(col == 0, sep[:width], sep[width:])
    middle = scale * middle
    lower = scale * lower
    a, b = outs
    head = a.shape[0] - unit
    put(a, slice(0, unit), sent)
    put(a, slice(unit, unit + head), sep[:head])
    rest = width - head
    put(b, slice(0, rest), sep[head:])
    put(b, slice(rest, rest + width), jnp.concatenate([middle[:width], middle[width:]], axis=1))
    put(b, slice(rest + width, rest + width + w2 // 2), jnp.concatenate([lower[: w2 // 2], lower[w2 // 2 :]], axis=1))


def tail_rows(unit, width, w2):
    half = (unit + 2 * width + w2 // 2) // 2
    return half, half - unit


def unit_call(where, weight, shards, split_factors, sums, ends, name):
    poles, rows, w0 = shards[0].shape
    w_high, w_low, l_high, l_low = split_factors
    lanes, w2 = w_high.shape[2], l_high.shape[2]
    w1 = lanes - w2
    unit = 2 * rows
    first_unit, last = not sums, bool(ends)

    def whole(x):
        return pl.BlockSpec((1,) + x.shape[1:], lambda p, w, t: (p, 0, 0))

    def kept(x):
        return pl.BlockSpec(x.shape, lambda p, w, t: (0, 0))

    f32 = jnp.float32
    gram = [jax.ShapeDtypeStruct((poles, lanes, w1), f32), jax.ShapeDtypeStruct((poles, w2, w2), f32)]
    if last:
        half, _ = tail_rows(unit, w1 // 2, w2)
        outs = [jax.ShapeDtypeStruct((half, w1), f32)] * 2
    elif first_unit:
        outs = [jax.ShapeDtypeStruct((unit, w1), f32)] * 2
    else:
        outs = [jax.ShapeDtypeStruct((rows, w1), f32)] * 2
    args = list(shards) + list(split_factors) + list(sums) + list(ends)
    out_specs = [kept(o) for o in outs]
    if not last:
        outs = outs + gram
        out_specs = out_specs + [whole(g) for g in gram]
    flops = 6 * poles * (unit * w0 * lanes + unit * w1 * lanes + unit * w2 * w2)
    return pl.pallas_call(
        functools.partial(unit_kernel, len(shards) // 2, first_unit, last, 2),
        grid_spec=pltpu.PrefetchScalarGridSpec(
            num_scalar_prefetch=2,
            grid=(poles,),
            in_specs=[whole(a) for a in args],
            out_specs=out_specs,
            scratch_shapes=[pltpu.VMEM((unit, w0), jnp.bfloat16)] * 2,
        ),
        out_shape=outs,
        compiler_params=pltpu.CompilerParams(vmem_limit_bytes=40 * MIB),
        cost_estimate=pl.CostEstimate(flops=flops, bytes_accessed=16 * MIB, transcendentals=0),
        name=name,
    )(where, weight, *args)


def place_kernel(unit, order, *refs):
    rows, w1 = unit // 2, refs[0].shape[1]
    width = w1 // 2
    root, off, upper = refs[-3:]

    def put(owner, at, value):
        here = pl.ds(pl.multiple_of(owner * unit + at, rows), value.shape[0])
        off[here] = value[:, :width]
        upper[here] = value[:, width:]

    put(order[0], 0, refs[0][...] + refs[1][...])
    total = refs[2][...] + refs[3][...]
    root[:, :w1] = total[:rows]
    root[:, w1:] = total[rows:]
    for k in range(1, (len(refs) - 3) // 4):
        put(order[k], 0, refs[4 * k][...] + refs[4 * k + 1][...])
        put(order[k], rows, refs[4 * k + 2][...] + refs[4 * k + 3][...])


def place(order, early, unit, w0, w2):
    w1 = early[0].shape[1]

    def whole(shape):
        return pl.BlockSpec(shape, lambda w: (0, 0))

    outs = [(unit // 2, w0), (w0, w1 // 2), (w0, w2)]
    return pl.pallas_call(
        functools.partial(place_kernel, unit),
        grid_spec=pltpu.PrefetchScalarGridSpec(
            num_scalar_prefetch=1,
            grid=(),
            in_specs=[pl.BlockSpec(memory_space=pltpu.VMEM)] * len(early),
            out_specs=[pl.BlockSpec(memory_space=pltpu.VMEM)] * 3,
        ),
        out_shape=[jax.ShapeDtypeStruct(o, jnp.float32) for o in outs],
        compiler_params=pltpu.CompilerParams(vmem_limit_bytes=24 * MIB),
        cost_estimate=pl.CostEstimate(flops=MIB, bytes_accessed=8 * MIB, transcendentals=0),
        name="place",
    )(order, *early)


def finish_kernel(unit, head, where, a, a_in, b, b_in, _off, _upper, off, upper, sep, middle, lower):
    total_a = a[...] + a_in[...]
    total_b = b[...] + b_in[...]
    width = off.shape[1]
    off[...] = total_a[:unit, :width]
    upper[...] = total_a[:unit, width:]
    sep[:head] = total_a[unit:]
    rest = width - head
    sep[head:] = total_b[:rest]
    w2 = lower.shape[1]
    middle[:width] = total_b[rest : rest + width, :w2]
    middle[width:] = total_b[rest : rest + width, w2:]
    lower[: w2 // 2] = total_b[rest + width :, :w2]
    lower[w2 // 2 :] = total_b[rest + width :, w2:]


def finish(where, late, off, upper, unit, w1, w2):
    width = w1 // 2
    half, head = tail_rows(unit, width, w2)
    piece = pl.BlockSpec((half, w1), lambda i, w: (0, 0))
    anywhere = pl.BlockSpec(memory_space=pl.ANY)

    def rows(x):
        return pl.BlockSpec((unit, x.shape[1]), lambda i, w: (w[1], 0))

    def whole(*shape):
        return pl.BlockSpec(shape, lambda i, w: (0, 0))

    shapes = [off.shape, upper.shape, (width, w1), (w1, w2), (w2, w2)]
    return pl.pallas_call(
        functools.partial(finish_kernel, unit, head),
        grid_spec=pltpu.PrefetchScalarGridSpec(
            num_scalar_prefetch=1,
            grid=(1,),
            in_specs=[piece] * 4 + [anywhere] * 2,
            out_specs=[rows(off), rows(upper)] + [whole(*s) for s in shapes[2:]],
        ),
        out_shape=[jax.ShapeDtypeStruct(s, jnp.float32) for s in shapes],
        input_output_aliases={5: 0, 6: 1},
        compiler_params=pltpu.CompilerParams(vmem_limit_bytes=24 * MIB),
        cost_estimate=pl.CostEstimate(flops=MIB, bytes_accessed=6 * MIB, transcendentals=0),
        name="finish",
    )(where, *late, off, upper)


def line_plan(n):
    plan = []
    for j in range(n):
        above = [(j % 2, s, j + s) for s in range(1, n - j)]
        below = [(1 - j % 2, s, j - s) for s in range(1, j + 1)]
        plan.append(sorted(above + below, key=lambda e: (e[1], e[0])))
    return plan


def line_pairs(n, kind, slot):
    pairs = []
    for k in range(kind, n - 1, 2):
        if k - slot + 1 >= 0:
            pairs.append((k, k + 1))
        if k + slot <= n - 1:
            pairs.append((k + 1, k))
    return pairs


def pole_pairs(n, bit):
    return [(p, p ^ bit) for p in range(n)]


def pole_step(a, b, n_pole, step):
    bits = [1 << i for i in range(n_pole.bit_length() - 1)]
    return (
        lax.ppermute(a, "pole", pole_pairs(n_pole, bits[step])),
        lax.ppermute(b, "pole", pole_pairs(n_pole, bits[-1 - step])),
    )


def together(*groups):
    flat, tree = jax.tree.flatten(groups)
    return jax.tree.unflatten(tree, lax.optimization_barrier(tuple(flat)))


def paired(
    n_pole,
    n_row,
    root_inverse,
    node_factor,
    node_inverse,
    leaf_root_factor,
    leaf_node_factor,
    leaf_inverse,
    leaf_pattern,
    pole_weight,
):
    row, col = lax.axis_index("row"), lax.axis_index("col")
    w0 = root_inverse.shape[2]
    w1, w2 = leaf_node_factor.shape[2:]
    unit = 2 * root_inverse.shape[1]
    steps = n_pole.bit_length() - 1
    plan = line_plan(n_row)
    entries = [[(0, 0, j) for j in range(n_row)]] + [[plan[j][k] for j in range(n_row)] for k in range(n_row - 1)]
    order = [jnp.array([e[2] for e in entry], jnp.int32)[row] for entry in entries]
    moved = {(0, 0): root_inverse, (1, 0): root_inverse}
    other = {}

    def swap(key):
        if key not in other:
            other[key] = lax.ppermute(moved[key], "col", SWAP)

    def advance(slot):
        for kind in range(2):
            pairs = line_pairs(n_row, kind, slot)
            if pairs:
                moved[kind, slot] = lax.ppermute(moved[1 - kind, slot - 1], "row", pairs)

    f_own = node_factor[:, 0]
    f_other = lax.ppermute(f_own, "col", SWAP)
    factors = prepare(
        jnp.stack([col, row]).astype(jnp.int32), leaf_pattern, f_own, f_other, leaf_root_factor[:, 0], leaf_node_factor[:, 0]
    )
    sums, early, waiting = [], [], []
    for k in range(n_row):
        kinds = sorted({e[:2] for e in entries[k]})
        for kind in kinds:
            swap(kind)
        if k < n_row - 1:
            advance(k + 1)
        choice = jnp.array([kinds.index(e[:2]) for e in entries[k]], jnp.int32)[row]
        where = jnp.stack([col.astype(jnp.int32), order[k], choice])
        shards = [s for kind in kinds for s in (moved[kind], other[kind])]
        last = k == n_row - 1
        ends = [node_inverse[:, 0], leaf_node_factor[:, 0], leaf_inverse[:, 0]] if last else []
        outs = unit_call(where, pole_weight, shards, factors, sums, ends, "unit")
        sums = list(outs[2:])
        a, b = outs[:2]
        if not last:
            moved, other, sums, a, b, early = together(moved, other, sums, a, b, early)
        late = []
        for step in range(steps):
            a_in, b_in = pole_step(a, b, n_pole, step)
            if step < steps - 1:
                a, b = a + a_in, b + b_in
        if not last:
            early += [a, a_in, b, b_in]
    late = [a, a_in, b, b_in]
    root, off, upper = place(jnp.stack(order), early, unit, w0, w2)
    off, upper, sep, middle, lower = finish(where, late, off, upper, unit, w1, w2)
    return root, off[None], sep[None], upper[None], middle[None], lower[None]


def solution(mesh):
    n_pole, n_row, n_col = (mesh.shape[axis] for axis in ("pole", "row", "col"))

    def shards(root_inverse, node_factor, *rest):
        fits = n_col == 2 and n_row == 4 and n_pole > 1 and n_pole & (n_pole - 1) == 0
        form = functools.partial(paired, n_pole, n_row) if fits else general
        return form(root_inverse, node_factor, *rest)

    return jax.shard_map(
        shards,
        mesh=mesh,
        in_specs=(
            P("pole", ("row", "col"), None),
            P("pole", "row", None, "col"),
            P("pole", "row", None, None),
            P("pole", ("row", "col"), None, None),
            P("pole", ("row", "col"), None, None),
            P("pole", ("row", "col"), None, None),
            P(("row", "col"), None),
            P("pole"),
        ),
        out_specs=(
            P(("row", "col"), None),
            P("row", None, "col"),
            P("row", "col", None),
            P(("row", "col"), None, None),
            P(("row", "col"), None, None),
            P(("row", "col"), None, None),
        ),
        check_vma=False,
    )
```

```python
import functools

import jax
import jax.numpy as jnp
from jax import lax
from jax.experimental import pallas as pl
from jax.experimental.pallas import tpu as pltpu
from jax.sharding import PartitionSpec as P

HIGH = lax.Precision.HIGH
SWAP = [(0, 1), (1, 0)]
MIB = 1 << 20


def product(left, right):
    return jnp.matmul(left, right, precision=HIGH)


def left_t(left, right):
    return jnp.einsum("pki,pkj->pij", left, right, precision=HIGH)


def weighted(weights, values):
    return jnp.sum(weights[:, None, None] * values, axis=0)


def general(
    root_inverse,
    node_factor,
    node_inverse,
    leaf_root_factor,
    leaf_node_factor,
    leaf_inverse,
    leaf_pattern,
    pole_weight,
):
    inv_n, leaf_n, inv_l = node_inverse[:, 0], leaf_node_factor[:, 0], leaf_inverse[:, 0]
    w1, width = inv_n.shape[2], node_factor.shape[3]
    start = lax.axis_index("col") * width
    row_mask = jnp.repeat(leaf_pattern[0].astype(jnp.float32), leaf_root_factor.shape[2] // leaf_pattern.shape[1])
    leaf = leaf_root_factor[:, 0] * row_mask[None, :, None]
    factor = lax.all_gather(node_factor[:, 0], "col", axis=2, tiled=True)
    root = lax.all_gather(root_inverse, ("row", "col"), axis=1, tiled=True)
    x = product(root, jnp.concatenate([factor, leaf - product(factor, leaf_n)], axis=2))
    gram = left_t(jnp.concatenate([factor, leaf], axis=2), x)
    sep = inv_n + gram[:, :w1, :w1]
    middle = jnp.swapaxes(gram[:, w1:, :w1], 1, 2) - product(sep, leaf_n)
    lower = inv_l + gram[:, w1:, w1:] - left_t(leaf_n, middle)
    rows = -weighted(pole_weight, x)
    totals = lax.psum(
        (
            weighted(pole_weight, root_inverse),
            lax.dynamic_slice_in_dim(rows, start, width, 1),
            lax.dynamic_slice_in_dim(weighted(pole_weight, sep), start, width, 0),
            rows[:, w1:],
            weighted(pole_weight, middle),
            weighted(pole_weight, lower),
        ),
        "pole",
    )
    return (totals[0],) + tuple(t[None] for t in totals[1:])


VMEM = pl.BlockSpec(memory_space=pltpu.VMEM)
SMEM = pl.BlockSpec(memory_space=pltpu.SMEM)
ACROSS = ((0,), (0,))


def call(kernel, name, outs, args, smem, **options):
    return pl.pallas_call(
        kernel,
        in_specs=[SMEM] * smem + [VMEM] * (len(args) - smem),
        out_specs=[VMEM] * len(outs),
        out_shape=outs,
        compiler_params=pltpu.CompilerParams(vmem_limit_bytes=20 * MIB),
        cost_estimate=pl.CostEstimate(flops=1, bytes_accessed=1, transcendentals=0),
        name=name,
        **options,
    )(*args)


def split(x):
    high = x.astype(jnp.bfloat16)
    return high, (x - high.astype(jnp.float32)).astype(jnp.bfloat16)


def dot3(left, right, dims=((1,), (0,))):
    def one(a, b):
        return lax.dot_general(a, b, (dims, ((), ())), preferred_element_type=jnp.float32)

    return one(left[0], right[0]) + (one(left[0], right[1]) + one(left[1], right[0]))


def pick(table, row):
    value = jnp.int32(table[0])
    for j in range(1, len(table)):
        value = jnp.where(row == j, table[j], value)
    return value


def prepare_kernel(
    where, pattern, f_other, f_hbm, leaf_hbm, leaf_n_hbm, w_high, w_low, l_high, l_low, f_own, leaf, leaf_n, sems, n_sems
):
    poles, w0, width = f_own.shape
    w1 = 2 * width
    block = w0 // pattern.shape[1]
    rows = w0 // sems.shape[1]
    first = where[0] == 0

    def copies(p, i):
        here = pl.ds(i * rows, rows)
        return [
            pltpu.make_async_copy(hbm.at[p, here], ref.at[p, here], sems.at[p, i, j])
            for j, (hbm, ref) in enumerate([(f_hbm, f_own), (leaf_hbm, leaf)])
        ]

    def copy_n(p):
        return pltpu.make_async_copy(leaf_n_hbm.at[p], leaf_n.at[p], n_sems.at[p])

    for p in range(poles):
        copy_n(p).start()
        for i in range(w0 // rows):
            for copy in copies(p, i):
                copy.start()
    for p in range(poles):
        copy_n(p).wait()
        ns = split(leaf_n[p])
        for i in range(w0 // rows):
            for copy in copies(p, i):
                copy.wait()
            here = pl.ds(i * rows, rows)
            own, other = f_own[p, here], f_other[p, here]
            f = jnp.concatenate([jnp.where(first, own, other), jnp.where(first, other, own)], axis=1)
            masked = leaf[p, here]
            kept = []
            for j in range(0, rows, block):
                kept.append(jnp.where(pattern[0, (i * rows + j) // block] != 0, masked[j : j + block], 0.0))
            masked = jnp.concatenate(kept, axis=0)
            fs = split(f)
            ds = split(masked - dot3(fs, ns))
            w_high[p, here, :w1], w_low[p, here, :w1] = fs
            w_high[p, here, w1:], w_low[p, here, w1:] = ds
            l_high[p, here], l_low[p, here] = split(masked)


def prepare(where, pattern, f_own, f_other, leaf, leaf_n):
    poles, w0, width = f_own.shape
    w1, w2 = leaf_n.shape[1:]
    parts = 4
    hbm = [pltpu.with_memory_space_constraint(x, pltpu.HBM) for x in (f_own, leaf, leaf_n)]
    return pl.pallas_call(
        prepare_kernel,
        in_specs=[SMEM] * 2 + [VMEM] + [pl.BlockSpec(memory_space=pltpu.HBM)] * 3,
        out_specs=[VMEM] * 4,
        out_shape=[pltpu.VMEM((poles, w0, n), jnp.bfloat16) for n in (w1 + w2, w1 + w2, w2, w2)],
        scratch_shapes=[
            pltpu.VMEM((poles, w0, width), jnp.float32),
            pltpu.VMEM((poles, w0, w2), jnp.float32),
            pltpu.VMEM((poles, w1, w2), jnp.float32),
            pltpu.SemaphoreType.DMA((poles, parts, 2)),
            pltpu.SemaphoreType.DMA((poles,)),
        ],
        compiler_params=pltpu.CompilerParams(vmem_limit_bytes=20 * MIB),
        cost_estimate=pl.CostEstimate(flops=1, bytes_accessed=1, transcendentals=0),
        name="prepare",
    )(where, pattern, f_other, *hbm)


def unit_kernel(form, slots, owners, slot_of, ways, where, weight, *refs):
    count = {"first": 1, "next": 2, "part": 1, "last": 1}[form]
    shards, refs = refs[: 2 * slots * count], refs[2 * slots * count :]
    (w_high, w_low, l_high, l_low), refs = refs[:4], refs[4:]
    if form in ("next", "last"):
        (gram_in, square_in), refs = refs[:2], refs[2:]
    if form == "last":
        (kept_rows, kept_high, kept_low, inv_n, leaf_n, inv_l), refs = refs[:6], refs[6:]
    if form == "last":
        outs, (r_high, r_low, sent_at, rest_at) = refs[:-4], refs[-4:]
    else:
        outs, (r_high, r_low) = refs[:-2], refs[-2:]
    col, row = where[0], where[1]
    owner, slot, way = (pick(table, row) for table in (owners, slot_of, ways))
    poles, rows, _ = shards[0].shape
    w2 = l_high.shape[2]
    w1 = w_high.shape[2] - w2
    width = w1 // 2
    begin = [pl.multiple_of(jnp.where(way == i, 0, rows), rows) for i in range(2)]
    if form == "first":
        for i in range(2):
            at = pl.ds(pl.multiple_of(jnp.where(col == i, 0, rows), rows), rows)
            for p in range(poles):
                r_high[p, at], r_low[p, at] = split(shards[i][p])
    else:
        for i in range(count):
            at = pl.ds(begin[i] if count == 2 else 0, rows)
            for s in range(slots):
                for j in range(2):
                    ref = shards[(2 * s + j) * count + i]

                    @pl.when((slot == s) & ((way == col) == (j == 0)))
                    def _():
                        for p in range(poles):
                            r_high[p, at], r_low[p, at] = split(ref[p])

    span = r_high.shape[1]
    base = owner * 2 * rows
    if form == "last":
        heres = [pl.ds(pl.multiple_of(base + begin[i], rows), rows) for i in range(2)]
    else:
        heres = [pl.ds(pl.multiple_of(base, 2 * rows), span)]
    for p in range(poles):
        x = dot3((r_high[p], r_low[p]), (w_high[p], w_low[p]))
        scale = weight[p]
        mine = jnp.where(col == 0, x[:, :width], x[:, width:w1])
        sent = -scale * jnp.concatenate([mine, x[:, w1:]], axis=1)
        sent_ref = sent_at if form == "last" else outs[0]
        if p == 0:
            sent_ref[...] = sent
        else:
            sent_ref[...] += sent
        xs = split(x)
        if form == "part":
            outs[1][p], outs[2][p] = xs
            continue
        if form == "last":
            xs = [jnp.concatenate([kept[p], v], axis=0) for kept, v in zip((kept_high, kept_low), xs)]
        fs = [jnp.concatenate([w[p, here, :w1] for here in heres], axis=0) for w in (w_high, w_low)]
        ls = [jnp.concatenate([l[p, here] for here in heres], axis=0) for l in (l_high, l_low)]
        ps = [v[:, :w1] for v in xs]
        us = [v[:, w1:] for v in xs]
        cross = dot3(fs, ps, ACROSS)
        below = dot3(ls, ps, ACROSS)
        inner = dot3(ls, us, ACROSS)
        if form != "first":
            cross = cross + gram_in[p, :w1]
            below = below + gram_in[p, w1:]
            inner = inner + square_in[p]
        if form != "last":
            gram, square = outs[-2:]
            gram[p, :w1] = cross
            gram[p, w1:] = below
            square[p] = inner
            continue
        sep = inv_n[p] + cross
        ns = split(leaf_n[p])
        middle = below.T - dot3(split(sep), ns)
        lower = inv_l[p] + inner - dot3(ns, split(middle), ACROSS)
        sep = scale * jnp.where(col == 0, sep[:width], sep[width:])
        middle = scale * jnp.concatenate([middle[:width], middle[width:]], axis=1)
        lower = scale * jnp.concatenate([lower[: w2 // 2], lower[w2 // 2 :]], axis=1)
        value = jnp.concatenate([sep, middle, lower], axis=0)
        if p == 0:
            rest_at[...] = value
        else:
            rest_at[...] += value
    if form == "last":
        keep, send = outs
        head = keep.shape[0] - 2 * rows
        for i, halves in enumerate([(keep, send), (send, keep)]):

            @pl.when(where[2] == i)
            def _():
                halves[0][:rows] = kept_rows[...]
                halves[0][rows : 2 * rows] = sent_at[...]
                halves[0][2 * rows :] = rest_at[:head]
                halves[1][...] = rest_at[head:]


def unit_call(form, tables, where, weight, shards, factors, sums=(), ends=()):
    poles, rows, w0 = shards[0].shape
    lanes, w2 = factors[0].shape[2], factors[2].shape[2]
    w1 = lanes - w2
    f32 = jnp.float32
    gram = [pltpu.VMEM((poles, lanes, w1), f32), pltpu.VMEM((poles, w2, w2), f32)]
    outs = {
        "first": [pltpu.VMEM((2 * rows, w1), f32)] + gram,
        "next": [pltpu.VMEM((2 * rows, w1), f32)] + gram,
        "part": [pltpu.VMEM((rows, w1), f32)] + [pltpu.VMEM((poles, rows, lanes), jnp.bfloat16)] * 2,
        "last": [pltpu.VMEM(((2 * rows + w1 // 2 + w1 // 2 + w2 // 2) // 2, w1), f32)] * 2,
    }[form]
    args = [where, weight, *shards, *factors, *sums, *ends]
    slots = len(shards) // (4 if form == "next" else 2)
    span = rows * (2 if form in ("first", "next") else 1)
    options = {"scratch_shapes": [pltpu.VMEM((poles, span, w0), jnp.bfloat16)] * 2}
    if form == "last":
        options["scratch_shapes"] += [pltpu.VMEM((rows, w1), f32), pltpu.VMEM((w1 + w2 // 2, w1), f32)]
    if form == "next":
        options["input_output_aliases"] = {len(args) - 2: 1, len(args) - 1: 2}
    return list(call(functools.partial(unit_kernel, form, slots, *tables), form, outs, args, 2, **options))


def place_kernel(unit, owners, pieces, where, *refs):
    sums, (root, off, upper) = refs[:-3], refs[-3:]
    width = off.shape[1]
    for pair, start, rows, k, at in pieces:
        here = pl.ds(start, rows)
        total = sums[2 * pair][here] + sums[2 * pair + 1][here]
        if k is None:
            root[:, at : at + total.shape[1]] = total
            continue
        there = pl.ds(pl.multiple_of(pick(owners[k], where[1]) * unit + at, unit // 2), rows)
        off[there] = total[:, :width]
        upper[there] = total[:, width:]


def place(owners, pieces, where, sums, unit, w0, w2):
    w1 = sums[0].shape[1]
    outs = [jax.ShapeDtypeStruct(o, jnp.float32) for o in [(unit // 2, w0), (w0, w1 // 2), (w0, w2)]]
    return call(functools.partial(place_kernel, unit, owners, pieces), "place", outs, [where, *sums], 1)


def finish_kernel(unit, owners, ways, where, kept, got, _off, _upper, off, upper, sep, middle, lower, *scratch):
    off_part, upper_part, sem = scratch
    rows = unit // 2
    width = off.shape[1]
    w2 = lower.shape[1]
    head = kept.shape[0] - unit
    base, way = (pick(table, where[1]) for table in (owners, ways))
    copies = []
    for i in range(2):
        here = pl.ds(i * rows, rows)
        there = pl.ds(pl.multiple_of(base * unit + jnp.where(way == i, 0, rows), rows), rows)
        for part, out in [(off_part, off), (upper_part, upper)]:
            copies.append(pltpu.make_async_copy(part.at[here], out.at[there], sem.at[len(copies)]))
    for i, (a, b) in enumerate([(kept, got), (got, kept)]):

        @pl.when(where[2] == i)
        def _():
            off_part[...] = a[:unit, :width]
            upper_part[...] = a[:unit, width:]
            sep[:head] = a[unit:]
            sep[head:] = b[: width - head]
            at = width - head
            middle[:width] = b[at : at + width, :w2]
            middle[width:] = b[at : at + width, w2:]
            at += width
            lower[: w2 // 2] = b[at:, :w2]
            lower[w2 // 2 :] = b[at:, w2:]

    for copy in copies:
        copy.start()
    for copy in copies:
        copy.wait()


def finish(tables, where, kept, got, off, upper, unit, w1, w2):
    anywhere = pl.BlockSpec(memory_space=pl.ANY)
    shapes = [off.shape, upper.shape, (w1 // 2, w1), (w1, w2), (w2, w2)]
    return pl.pallas_call(
        functools.partial(finish_kernel, unit, *tables),
        in_specs=[SMEM] + [VMEM] * 2 + [anywhere] * 2,
        out_specs=[anywhere] * 2 + [VMEM] * 3,
        out_shape=[jax.ShapeDtypeStruct(s, jnp.float32) for s in shapes],
        scratch_shapes=[
            pltpu.VMEM((unit, w1 // 2), jnp.float32),
            pltpu.VMEM((unit, w2), jnp.float32),
            pltpu.SemaphoreType.DMA((4,)),
        ],
        input_output_aliases={3: 0, 4: 1},
        compiler_params=pltpu.CompilerParams(vmem_limit_bytes=20 * MIB),
        cost_estimate=pl.CostEstimate(flops=1, bytes_accessed=1, transcendentals=0),
        name="finish",
    )(where, kept, got, off, upper)


def line_plan(n):
    plan = []
    for j in range(n):
        above = [(s, 0, j + s) for s in range(1, n - j)]
        below = [(s, 1, j - s) for s in range(1, j + 1)]
        plan.append(sorted(above + below, key=lambda e: (e[0], e[1] if j < n // 2 else -e[1])))
    return plan


def together(*groups):
    flat, tree = jax.tree.flatten(groups)
    return jax.tree.unflatten(tree, lax.optimization_barrier(tuple(flat)))


def paired(
    n_pole,
    n_row,
    root_inverse,
    node_factor,
    node_inverse,
    leaf_root_factor,
    leaf_node_factor,
    leaf_inverse,
    leaf_pattern,
    pole_weight,
):
    pole, col = lax.axis_index("pole"), lax.axis_index("col")
    where = jnp.stack([col, lax.axis_index("row"), jnp.where(col == 0, pole & 1, pole // 2)]).astype(jnp.int32)
    w0 = root_inverse.shape[2]
    w1, w2 = leaf_node_factor.shape[2:]
    own_rows = root_inverse.shape[1]
    unit = 2 * own_rows
    units = [[(0, 0, j) for j in range(n_row)]] + [list(unit) for unit in zip(*line_plan(n_row))]
    slots = [sorted({e[0] for e in unit}) for unit in units]
    tables = [
        ([e[2] for e in unit], [slot.index(e[0]) for e in unit], [e[1] for e in unit]) for unit, slot in zip(units, slots)
    ]
    owners = [table[0] for table in tables]
    moved, other = {}, {}

    def advance(slot, i):
        down = [(2 * j, 2 * (j - 1)) for j in range(1, n_row - slot + 1)]
        up = [(2 * j + 1, 2 * j + 3) for j in range(slot - 1, n_row - 1)]
        moved[slot, i] = lax.ppermute(moved[slot - 1, i], ("row", "col"), down + up)

    def swap(key):
        other[key] = lax.ppermute(moved[key], "col", SWAP)

    token = pole_weight

    def hold(keys, *rest):
        nonlocal token
        got, over, token, rest = together(
            [moved[key] for key in keys], [other[key] for key in keys if key in other], token, rest
        )
        moved.update(zip(keys, got, strict=True))
        other.update(zip([key for key in keys if key in other], over, strict=True))
        return rest

    def step(value, turn):
        pairs = [(2 * p + c, 2 * (p ^ (1 << (c ^ turn))) + c) for p in range(n_pole) for c in range(2)]
        return lax.ppermute(value, ("pole", "col"), pairs)

    def cut(pair, rows):
        return pair[0][:rows] + pair[1][:rows]

    def unit_of(form, k, which, *rest):
        shards = [held[slot, i] for slot in slots[k] for held in (moved, other) for i in which]
        return unit_call(form, tables[k], where, token, shards, *rest)

    f_own = node_factor[:, 0]
    f_other = lax.ppermute(f_own, "col", SWAP)
    moved[0, 0] = root_inverse
    advance(1, 0)
    swap((0, 0))
    moved[0, 1] = other[0, 0]
    advance(1, 1)
    root = weighted(pole_weight, root_inverse)
    root = jnp.concatenate([root[:, :w1], root[:, w1:]], axis=0)
    roots = (root, step(root, 0))
    factors = prepare(where, leaf_pattern, f_own, f_other, leaf_root_factor[:, 0], leaf_node_factor[:, 0])

    (factors,) = hold([(1, 0)], factors)
    swap((1, 0))
    advance(2, 0)
    rows, *sums = unit_of("first", 0, (0,), factors)
    rows, sums = hold([(1, 1)], rows, sums)
    (roots,) = hold([], roots)
    value = jnp.concatenate([rows, roots[0] + roots[1]], axis=0)
    first = (value, step(value, 1))
    swap((1, 1))
    advance(2, 1)
    hold([(1, 0)])

    hold([(2, 0)])
    swap((2, 0))
    advance(3, 0)
    (first,) = hold([], first)
    hold([(1, 1)])
    rows, *sums = unit_of("next", 1, (0, 1), factors, sums)
    rows, sums = hold([], rows, sums)
    value = jnp.concatenate([rows, cut(first, unit)], axis=0)
    second = (value, step(value, 0))

    hold([(2, 1)])
    swap((2, 1))
    advance(3, 1)
    hold([(2, 0)])

    hold([(3, 0)])
    swap((3, 0))
    (second,) = hold([], second)
    value = cut(second, unit)
    third = (value, step(value, 1))
    hold([(2, 1)])
    rows, *sums = unit_of("next", 2, (0, 1), factors, sums)
    rows, sums = hold([], rows, sums)
    fourth = (rows, step(rows, 0))

    hold([(3, 1)])
    swap((3, 1))
    hold([(3, 0)])
    kept = unit_of("part", 3, (0,), factors)
    (third,) = hold([], third)
    fourth, kept = hold([], fourth, kept)
    value = cut(fourth, unit)
    fifth = (value, step(value, 1))
    hold([(3, 1)])
    ends = (*kept, node_inverse[:, 0], leaf_node_factor[:, 0], leaf_inverse[:, 0])
    keep, send = unit_of("last", 3, (1,), factors, sums, ends)
    got = step(send, 0)
    pieces = [(0, unit, own_rows, None, 0), (0, unit + own_rows, own_rows, None, w1), (1, unit, unit, 0, 0)]
    pieces += [(2, 0, unit, 1, 0), (3, 0, unit, 2, 0)]
    early = [v for pair in (first, second, third, fifth) for v in pair]
    root, off, upper = place(owners, pieces, where, early, unit, w0, w2)
    keep, got, root, off, upper = hold([], keep, got, root, off, upper)
    keep = keep + got
    keep = keep + step(keep, 1)
    got = step(keep, 0)
    off, upper, sep, middle, lower = finish(tables[3][::2], where, keep, got, off, upper, unit, w1, w2)
    return root, off[None], sep[None], upper[None], middle[None], lower[None]


def solution(mesh):
    n_pole, n_row, n_col = (mesh.shape[axis] for axis in ("pole", "row", "col"))

    def shards(root_inverse, node_factor, *rest):
        fits = n_col == 2 and n_row == 4 and n_pole == 4
        form = functools.partial(paired, n_pole, n_row) if fits else general
        return form(root_inverse, node_factor, *rest)

    return jax.shard_map(
        shards,
        mesh=mesh,
        in_specs=(
            P("pole", ("row", "col"), None),
            P("pole", "row", None, "col"),
            P("pole", "row", None, None),
            P("pole", ("row", "col"), None, None),
            P("pole", ("row", "col"), None, None),
            P("pole", ("row", "col"), None, None),
            P(("row", "col"), None),
            P("pole"),
        ),
        out_specs=(
            P(("row", "col"), None),
            P("row", None, "col"),
            P("row", "col", None),
            P(("row", "col"), None, None),
            P(("row", "col"), None, None),
            P(("row", "col"), None, None),
        ),
        check_vma=False,
    )
```

```python
import functools

import jax
import jax.numpy as jnp
from jax import lax
from jax.experimental import pallas as pl
from jax.experimental.pallas import tpu as pltpu
from jax.sharding import PartitionSpec as P

HIGH = lax.Precision.HIGH
SWAP = [(0, 1), (1, 0)]
MIB = 1 << 20


def product(left, right):
    return jnp.matmul(left, right, precision=HIGH)


def left_t(left, right):
    return jnp.einsum("pki,pkj->pij", left, right, precision=HIGH)


def weighted(weights, values):
    return jnp.sum(weights[:, None, None] * values, axis=0)


def general(
    root_inverse,
    node_factor,
    node_inverse,
    leaf_root_factor,
    leaf_node_factor,
    leaf_inverse,
    leaf_pattern,
    pole_weight,
):
    inv_n, leaf_n, inv_l = node_inverse[:, 0], leaf_node_factor[:, 0], leaf_inverse[:, 0]
    w1, width = inv_n.shape[2], node_factor.shape[3]
    start = lax.axis_index("col") * width
    row_mask = jnp.repeat(leaf_pattern[0].astype(jnp.float32), leaf_root_factor.shape[2] // leaf_pattern.shape[1])
    leaf = leaf_root_factor[:, 0] * row_mask[None, :, None]
    factor = lax.all_gather(node_factor[:, 0], "col", axis=2, tiled=True)
    root = lax.all_gather(root_inverse, ("row", "col"), axis=1, tiled=True)
    x = product(root, jnp.concatenate([factor, leaf - product(factor, leaf_n)], axis=2))
    gram = left_t(jnp.concatenate([factor, leaf], axis=2), x)
    sep = inv_n + gram[:, :w1, :w1]
    middle = jnp.swapaxes(gram[:, w1:, :w1], 1, 2) - product(sep, leaf_n)
    lower = inv_l + gram[:, w1:, w1:] - left_t(leaf_n, middle)
    rows = -weighted(pole_weight, x)
    totals = lax.psum(
        (
            weighted(pole_weight, root_inverse),
            lax.dynamic_slice_in_dim(rows, start, width, 1),
            lax.dynamic_slice_in_dim(weighted(pole_weight, sep), start, width, 0),
            rows[:, w1:],
            weighted(pole_weight, middle),
            weighted(pole_weight, lower),
        ),
        "pole",
    )
    return (totals[0],) + tuple(t[None] for t in totals[1:])


VMEM = pl.BlockSpec(memory_space=pltpu.VMEM)
SMEM = pl.BlockSpec(memory_space=pltpu.SMEM)
ACROSS = ((0,), (0,))


def call(kernel, name, outs, args, smem, **options):
    return pl.pallas_call(
        kernel,
        in_specs=[SMEM] * smem + [VMEM] * (len(args) - smem),
        out_specs=[VMEM] * len(outs),
        out_shape=outs,
        compiler_params=pltpu.CompilerParams(vmem_limit_bytes=20 * MIB),
        cost_estimate=pl.CostEstimate(flops=1, bytes_accessed=1, transcendentals=0),
        name=name,
        **options,
    )(*args)


def split(x):
    high = x.astype(jnp.bfloat16)
    return high, (x - high.astype(jnp.float32)).astype(jnp.bfloat16)


def dot3(left, right, dims=((1,), (0,))):
    def one(a, b):
        return lax.dot_general(a, b, (dims, ((), ())), preferred_element_type=jnp.float32)

    k = dims[0][0]
    return one(
        jnp.concatenate([left[0], left[0], left[1]], axis=k), jnp.concatenate([right[0], right[1], right[0]], axis=0)
    )


def pick(table, row):
    value = jnp.int32(table[0])
    for j in range(1, len(table)):
        value = jnp.where(row == j, table[j], value)
    return value


def prepare_kernel(
    where, pattern, f_other, f_hbm, leaf_hbm, leaf_n_hbm, w_high, w_low, l_high, l_low, f_own, leaf, leaf_n, sems, n_sems
):
    poles, w0, width = f_own.shape
    w1 = 2 * width
    block = w0 // pattern.shape[1]
    rows = w0 // sems.shape[1]
    first = where[0] == 0

    def copies(p, i):
        here = pl.ds(i * rows, rows)
        return [
            pltpu.make_async_copy(hbm.at[p, here], ref.at[p, here], sems.at[p, i, j])
            for j, (hbm, ref) in enumerate([(f_hbm, f_own), (leaf_hbm, leaf)])
        ]

    def copy_n(p):
        return pltpu.make_async_copy(leaf_n_hbm.at[p], leaf_n.at[p], n_sems.at[p])

    for p in range(poles):
        copy_n(p).start()
        for i in range(w0 // rows):
            for copy in copies(p, i):
                copy.start()
    for p in range(poles):
        copy_n(p).wait()
        ns = split(leaf_n[p])
        for i in range(w0 // rows):
            for copy in copies(p, i):
                copy.wait()
            here = pl.ds(i * rows, rows)
            own, other = f_own[p, here], f_other[p, here]
            f = jnp.concatenate([jnp.where(first, own, other), jnp.where(first, other, own)], axis=1)
            masked = leaf[p, here]
            kept = []
            for j in range(0, rows, block):
                kept.append(jnp.where(pattern[0, (i * rows + j) // block] != 0, masked[j : j + block], 0.0))
            masked = jnp.concatenate(kept, axis=0)
            fs = split(f)
            ds = split(masked - dot3(fs, ns))
            w_high[p, here, :w1], w_low[p, here, :w1] = fs
            w_high[p, here, w1:], w_low[p, here, w1:] = ds
            l_high[p, here], l_low[p, here] = split(masked)


def prepare(where, pattern, f_own, f_other, leaf, leaf_n):
    poles, w0, width = f_own.shape
    w1, w2 = leaf_n.shape[1:]
    parts = 4
    hbm = [pltpu.with_memory_space_constraint(x, pltpu.HBM) for x in (f_own, leaf, leaf_n)]
    return pl.pallas_call(
        prepare_kernel,
        in_specs=[SMEM] * 2 + [VMEM] + [pl.BlockSpec(memory_space=pltpu.HBM)] * 3,
        out_specs=[VMEM] * 4,
        out_shape=[pltpu.VMEM((poles, w0, n), jnp.bfloat16) for n in (w1 + w2, w1 + w2, w2, w2)],
        scratch_shapes=[
            pltpu.VMEM((poles, w0, width), jnp.float32),
            pltpu.VMEM((poles, w0, w2), jnp.float32),
            pltpu.VMEM((poles, w1, w2), jnp.float32),
            pltpu.SemaphoreType.DMA((poles, parts, 2)),
            pltpu.SemaphoreType.DMA((poles,)),
        ],
        compiler_params=pltpu.CompilerParams(vmem_limit_bytes=20 * MIB),
        cost_estimate=pl.CostEstimate(flops=1, bytes_accessed=1, transcendentals=0),
        name="prepare",
    )(where, pattern, f_other, *hbm)


def unit_kernel(form, slots, cuts, owners, slot_of, ways, where, weight, *refs):
    count = {"first": 1, "next": 2, "halves": 2, "part": 1, "last": 1}[form]
    shards = []
    for n in cuts:
        shards.append(refs[:n])
        refs = refs[n:]
    (w_high, w_low, l_high, l_low), refs = refs[:4], refs[4:]
    if form in ("next", "halves", "last"):
        (gram_in, square_in), refs = refs[:2], refs[2:]
    if form == "last":
        (kept_rows, kept_high, kept_low, inv_n), refs = refs[:4], refs[4:]
    if form == "last":
        outs, (r_high, r_low, sent_at, sep_at) = refs[:-4], refs[-4:]
    else:
        outs, (r_high, r_low) = refs[:-2], refs[-2:]
    col, row = where[0], where[1]
    owner, slot, way = (pick(table, row) for table in (owners, slot_of, ways))
    poles, rows, _ = shards[0][0].shape
    w2 = l_high.shape[2]
    w1 = w_high.shape[2] - w2
    width = w1 // 2
    begin = [pl.multiple_of(jnp.where(way == i, 0, rows), rows) for i in range(2)]
    if form == "first":
        for i in range(2):
            at = pl.ds(pl.multiple_of(jnp.where(col == i, 0, rows), rows), rows)
            for p in range(poles):
                r_high[p, at], r_low[p, at] = split(shards[i][0][p])
    else:
        for i in range(count):
            at = pl.ds(begin[i] if count == 2 else 0, rows)
            for s in range(slots):
                for j in range(2):
                    pieces = shards[(2 * s + j) * count + i]

                    @pl.when((slot == s) & ((way == col) == (j == 0)))
                    def _():
                        for p in range(poles):
                            piece = pieces[p * len(pieces) // poles]
                            r_high[p, at], r_low[p, at] = split(piece[p % piece.shape[0]])

    span = r_high.shape[1]
    base = owner * 2 * rows
    if form == "last":
        heres = [pl.ds(pl.multiple_of(base + begin[i], rows), rows) for i in range(2)]
    else:
        heres = [pl.ds(pl.multiple_of(base, 2 * rows), span)]
    for p in range(poles):
        x = dot3((r_high[p], r_low[p]), (w_high[p], w_low[p]))
        scale = weight[p]
        mine = jnp.where(col == 0, x[:, :width], x[:, width:w1])
        sent = -scale * jnp.concatenate([mine, x[:, w1:]], axis=1)
        sent_ref = sent_at if form == "last" else outs[0]
        if form == "halves":
            if p == 0:
                total = sent
            else:
                total = total + sent
        elif p == 0:
            sent_ref[...] = sent
        else:
            sent_ref[...] += sent
        xs = split(x)
        if form == "part":
            outs[1][p], outs[2][p] = xs
            continue
        if form == "last":
            xs = [jnp.concatenate([kept[p], v], axis=0) for kept, v in zip((kept_high, kept_low), xs)]
        fs = [jnp.concatenate([w[p, here, :w1] for here in heres], axis=0) for w in (w_high, w_low)]
        ls = [jnp.concatenate([l[p, here] for here in heres], axis=0) for l in (l_high, l_low)]
        ps = [v[:, :w1] for v in xs]
        us = [v[:, w1:] for v in xs]
        cross = dot3(fs, ps, ACROSS)
        below = dot3(ls, ps, ACROSS)
        inner = dot3(ls, us, ACROSS)
        if form != "first":
            cross = cross + gram_in[p, :w1]
            below = below + gram_in[p, w1:]
            inner = inner + square_in[p]
        gram, square = outs[-2:]
        gram[p, :w1] = cross
        gram[p, w1:] = below
        square[p] = inner
        if form == "last":
            sep = inv_n[p] + cross
            sep = scale * jnp.where(col == 0, sep[:width], sep[width:])
            if p == 0:
                sep_at[...] = sep
            else:
                sep_at[...] += sep
    if form == "halves":
        for i in range(2):

            @pl.when(where[2] == i)
            def _():
                outs[i][...] = total[:rows]
                outs[1 - i][...] = total[rows:]

    if form == "last":
        half = outs[0].shape[0]
        split_at = half - rows
        for i in range(2):

            @pl.when(where[2] == i)
            def _():
                outs[i][:rows] = kept_rows[...]
                outs[i][rows:] = sent_at[:split_at]
                outs[1 - i][: rows - split_at] = sent_at[split_at:]
                outs[1 - i][rows - split_at :] = sep_at[: half + split_at - rows]

        outs[2][...] = sep_at[half + split_at - rows :]


def ends_kernel(where, weight, gram, square, sep, inv_n, leaf_n, inv_l, keep, send, rest_at):
    poles, w1, w2 = leaf_n.shape
    width = w1 // 2
    start = sep.shape[0]
    rest_at[:start] = sep[...]
    for p in range(poles):
        ns = split(leaf_n[p])
        middle = gram[p, w1:].T - dot3(split(inv_n[p] + gram[p, :w1]), ns)
        lower = inv_l[p] + square[p] - dot3(ns, split(middle), ACROSS)
        middle = jnp.concatenate([middle[:width], middle[width:]], axis=1)
        lower = jnp.concatenate([lower[: w2 // 2], lower[w2 // 2 :]], axis=1)
        value = weight[p] * jnp.concatenate([middle, lower], axis=0)
        if p == 0:
            rest_at[start:] = value
        else:
            rest_at[start:] += value
    head = keep.shape[0]
    for i, (a, b) in enumerate([(keep, send), (send, keep)]):

        @pl.when(where[2] == i)
        def _():
            a[...] = rest_at[:head]
            b[...] = rest_at[head:]


def ends_call(where, weight, gram, square, sep, inv_n, leaf_n, inv_l):
    w1, w2 = leaf_n.shape[1:]
    rows = sep.shape[0] + (w1 + w2) // 2
    outs = [pltpu.VMEM((rows // 2, w1), jnp.float32)] * 2
    args = [where, weight, gram, square, sep, inv_n, leaf_n, inv_l]
    return call(ends_kernel, "ends", outs, args, 2, scratch_shapes=[pltpu.VMEM((rows, w1), jnp.float32)])


def halved(rows, w1, w2):
    quarter = (2 * rows + w1 + w2 // 2) // 4
    return (quarter + 0, quarter - 0), (112, rows - 112)


def unit_call(form, tables, where, weight, shards, factors, sums=(), ends=()):
    poles, rows, w0 = shards[0][0].shape
    lanes, w2 = factors[0].shape[2], factors[2].shape[2]
    w1 = lanes - w2
    f32 = jnp.float32
    head = halved(rows, w1, w2)[0][0]
    gram = [pltpu.VMEM((poles, lanes, w1), f32), pltpu.VMEM((poles, w2, w2), f32)]
    outs = {
        "first": [pltpu.VMEM((2 * rows, w1), f32)] + gram,
        "next": [pltpu.VMEM((2 * rows, w1), f32)] + gram,
        "halves": [pltpu.VMEM((rows, w1), f32)] * 2 + gram,
        "part": [pltpu.VMEM((rows, w1), f32)] + [pltpu.VMEM((poles, rows, lanes), jnp.bfloat16)] * 2,
        "last": [pltpu.VMEM((n, w1), f32) for n in (head, head, 2 * rows + w1 // 2 - 2 * head)] + gram,
    }[form]
    cuts = [len(pieces) for pieces in shards]
    args = [where, weight, *(x for pieces in shards for x in pieces), *factors, *sums, *ends]
    slots = len(shards) // (4 if form in ("next", "halves") else 2)
    span = rows * (1 if form in ("part", "last") else 2)
    options = {"scratch_shapes": [pltpu.VMEM((poles, span, w0), jnp.bfloat16)] * 2}
    if form == "last":
        options["scratch_shapes"] += [pltpu.VMEM((rows, w1), f32), pltpu.VMEM((w1 // 2, w1), f32)]
        at = len(args) - len(ends) - 2
        options["input_output_aliases"] = {at: 3, at + 1: 4}
    if form in ("next", "halves"):
        at = 2 if form == "halves" else 1
        options["input_output_aliases"] = {len(args) - 2: at, len(args) - 1: at + 1}
    return list(call(functools.partial(unit_kernel, form, slots, cuts, *tables), form, outs, args, 2, **options))


def place_kernel(unit, owners, pieces, where, *refs):
    sums, (root, off, upper) = refs[:-3], refs[-3:]
    width = off.shape[1]
    for pair, start, rows, k, at in pieces:
        here = pl.ds(start, rows)
        total = sums[2 * pair][here] + sums[2 * pair + 1][here]
        if k is None:
            root[:, at : at + total.shape[1]] = total
            continue
        there = pl.ds(pl.multiple_of(pick(owners[k], where[1]) * unit + at, unit // 2), rows)
        off[there] = total[:, :width]
        upper[there] = total[:, width:]


def place(owners, pieces, where, sums, unit, w0, w2):
    w1 = sums[0].shape[1]
    outs = [jax.ShapeDtypeStruct(o, jnp.float32) for o in [(unit // 2, w0), (w0, w1 // 2), (w0, w2)]]
    return call(functools.partial(place_kernel, unit, owners, pieces), "place", outs, [where, *sums], 1)


def finish_kernel(unit, halves, shares, part, table, owners, where, *refs):
    rows, half = unit // 2, halves[0]
    first, refs = refs[:2], refs[2:]
    if part:
        second, refs = refs[:2], refs[2:]
    (_, _, off, upper), refs = refs[:4], refs[4:]
    if part:
        (sep, middle, lower), refs = refs[:3], refs[3:]
    off_at, upper_at, sem = refs
    width = off.shape[1]
    base, way = (pick(t, where[1]) for t in table)
    before = pick(owners, where[1]) * unit
    places, start = [], 0
    for i, (a, b) in enumerate([first, first[::-1]]):

        @pl.when(where[2] == i)
        def _():
            if part == 0:
                for at, value in [(0, a[:half]), (half, b[: unit - half])]:
                    off_at[at : at + value.shape[0]] = value[:, :width]
                    upper_at[at : at + value.shape[0]] = value[:, width:]
                return
            c, d = second if i == 0 else second[::-1]
            w1, w2 = middle.shape
            rest = 2 * half - unit
            sep[:rest] = b[unit - half : half]
            sep[rest:] = c[: width - rest]
            end = halves[1]
            at = end - (width - rest)
            middle[:at] = c[width - rest : end, :w2]
            middle[width : width + at] = c[width - rest : end, w2:]
            middle[at:width] = d[: width - at, :w2]
            middle[width + at :] = d[: width - at, w2:]
            lower[: w2 // 2] = d[width - at : end, :w2]
            lower[w2 // 2 :] = d[width - at : end, w2:]

    if part == 0:
        places = [(i * rows, base * unit + jnp.where(way == i, 0, rows), rows) for i in range(2)]
        start = unit
    for i, ref in enumerate(second if part else first):
        size = shares[part]
        value = ref[halves[part] :]
        off_at[start : start + size] = value[:, :width]
        upper_at[start : start + size] = value[:, width:]
        places.append((start, before + jnp.where(where[2] == i, 0, rows) + part * shares[0], size))
        start += size
    copies = []
    for at, place, size in places:
        there = pl.ds(pl.multiple_of(place, 8), size)
        for value, out in [(off_at, off), (upper_at, upper)]:
            copies.append(pltpu.make_async_copy(value.at[pl.ds(at, size)], out.at[there], sem.at[len(copies)]))
    for copy in copies:
        copy.start()
    for copy in copies:
        copy.wait()


def finish(part, table, owners, where, sums, off, upper, unit, halves, shares, shapes=()):
    anywhere = pl.BlockSpec(memory_space=pl.ANY)
    rows = 2 * shares[part] + (0 if part else unit)
    outs = [off.shape, upper.shape, *shapes]
    at = 1 + len(sums)
    return pl.pallas_call(
        functools.partial(finish_kernel, unit, halves, shares, part, table, owners),
        in_specs=[SMEM] + [VMEM] * len(sums) + [anywhere] * 2,
        out_specs=[anywhere] * 2 + [VMEM] * len(shapes),
        out_shape=[jax.ShapeDtypeStruct(shape, jnp.float32) for shape in outs],
        scratch_shapes=[
            pltpu.VMEM((rows, off.shape[1]), jnp.float32),
            pltpu.VMEM((rows, upper.shape[1]), jnp.float32),
            pltpu.SemaphoreType.DMA((4 if part else 8,)),
        ],
        input_output_aliases={at: 0, at + 1: 1},
        compiler_params=pltpu.CompilerParams(vmem_limit_bytes=20 * MIB),
        cost_estimate=pl.CostEstimate(flops=1, bytes_accessed=1, transcendentals=0),
        name="finish",
    )(where, *sums, off, upper)


def line_plan(n):
    plan = []
    for j in range(n):
        above = [(s, 0, j + s) for s in range(1, n - j)]
        below = [(s, 1, j - s) for s in range(1, j + 1)]
        plan.append(sorted(above + below, key=lambda e: (e[0], e[1] if j < n // 2 else -e[1])))
    return plan


def together(*groups):
    flat, tree = jax.tree.flatten(groups)
    return jax.tree.unflatten(tree, lax.optimization_barrier(tuple(flat)))


def paired(
    n_pole,
    n_row,
    root_inverse,
    node_factor,
    node_inverse,
    leaf_root_factor,
    leaf_node_factor,
    leaf_inverse,
    leaf_pattern,
    pole_weight,
):
    pole, col = lax.axis_index("pole"), lax.axis_index("col")
    far = jnp.where(col == 0, pole // 2, pole & 1)
    where = jnp.stack([col, lax.axis_index("row"), far]).astype(jnp.int32)
    w0 = root_inverse.shape[2]
    w1, w2 = leaf_node_factor.shape[2:]
    own_rows = root_inverse.shape[1]
    unit = 2 * own_rows
    units = [[(0, 0, j) for j in range(n_row)]] + [list(unit) for unit in zip(*line_plan(n_row))]
    slots = [sorted({e[0] for e in unit}) for unit in units]
    tables = [
        ([e[2] for e in unit], [slot.index(e[0]) for e in unit], [e[1] for e in unit]) for unit, slot in zip(units, slots)
    ]
    owners = [table[0] for table in tables]
    moved, other = {}, {}

    def advance(slot, i):
        down = [(2 * j, 2 * (j - 1)) for j in range(1, n_row - slot + 1)]
        up = [(2 * j + 1, 2 * j + 3) for j in range(slot - 1, n_row - 1)]
        moved[slot, i] = lax.ppermute(moved[slot - 1, i], ("row", "col"), down + up)

    def swap(key, cuts=1):
        size = moved[key].shape[0] // cuts
        pieces = [moved[key][i * size : (i + 1) * size] for i in range(cuts)] if cuts > 1 else [moved[key]]
        other[key] = tuple(lax.ppermute(piece, "col", SWAP) for piece in pieces)

    token = pole_weight

    def hold(keys, *rest):
        nonlocal token
        got, over, token, rest = together(
            [moved[key] for key in keys], [other[key] for key in keys if key in other], token, rest
        )
        moved.update(zip(keys, got, strict=True))
        other.update(zip([key for key in keys if key in other], over, strict=True))
        return rest

    def step(value, turn):
        pairs = [(2 * p + c, 2 * (p ^ (1 << (c ^ turn))) + c) for p in range(n_pole) for c in range(2)]
        return lax.ppermute(value, ("pole", "col"), pairs)

    def cut(pair, rows):
        return pair[0][:rows] + pair[1][:rows]

    def unit_of(form, k, which, *rest):
        shards = []
        for slot in slots[k]:
            shards += [(moved[slot, i],) for i in which] + [other[slot, i] for i in which]
        return unit_call(form, tables[k], where, token, shards, *rest)

    f_own = node_factor[:, 0]
    f_other = lax.ppermute(f_own, "col", SWAP)
    moved[0, 0] = root_inverse
    advance(1, 0)
    swap((0, 0))
    (moved[0, 1],) = other[0, 0]
    advance(1, 1)
    factors = prepare(where, leaf_pattern, f_own, f_other, leaf_root_factor[:, 0], leaf_node_factor[:, 0])
    factors, root = together(factors, root_inverse)
    root = weighted(pole_weight, root)
    root = jnp.concatenate([root[:, :w1], root[:, w1:]], axis=0)
    roots = (root, step(root, 0))

    (factors,) = hold([(1, 0)], factors)
    swap((1, 0))
    advance(2, 0)
    rows, *sums = unit_of("first", 0, (0,), factors)
    rows, sums = hold([(1, 1)], rows, sums)
    (roots,) = hold([], roots)
    value = jnp.concatenate([rows, roots[0] + roots[1]], axis=0)
    first = (value, step(value, 1))
    swap((1, 1))
    advance(2, 1)
    hold([(1, 0)])

    hold([(2, 0)])
    swap((2, 0))
    advance(3, 0)
    (first,) = hold([], first)
    hold([(1, 1)])
    rows, *sums = unit_of("next", 1, (0, 1), factors, sums)
    rows, sums = hold([(2, 1)], rows, sums)
    value = jnp.concatenate([rows, cut(first, unit)], axis=0)
    swap((2, 1))
    second = (value, step(value, 0))
    advance(3, 1)
    hold([(2, 0)])

    hold([(3, 0)])
    swap((3, 0), 2)
    hold([(2, 1)])
    keep3, send3, *sums = unit_of("halves", 2, (0, 1), factors, sums)
    keep3, send3, sums, second = hold([], keep3, send3, sums, second)
    value = jnp.concatenate([cut(second, unit), send3], axis=0)
    third = (value, step(value, 1))

    hold([(3, 0)])
    kept = unit_of("part", 3, (0,), factors)
    (kept,) = hold([(3, 1)], kept)
    swap((3, 1))
    hold([(3, 1)])
    inv_n = node_inverse[:, 0]
    keep, send, rest, *sums = unit_of("last", 3, (1,), factors, sums, (*kept, inv_n))
    keep, send, rest, sums = hold([], keep, send, rest, sums)
    got = step(send, 1)
    keep2, send2 = ends_call(where, token, *sums, rest, inv_n, leaf_node_factor[:, 0], leaf_inverse[:, 0])
    keep2, send2, keep3, third = hold([], keep2, send2, keep3, third)
    got2 = step(send2, 1)
    keep3 = keep3 + third[1][unit:]
    halves, shares = halved(own_rows, w1, w2)
    keep, got = hold([], keep, got)
    keep = jnp.concatenate([keep + got, keep3[: shares[0]]], axis=0)
    got = step(keep, 0)
    keep2, got2 = hold([], keep2, got2)
    keep2 = jnp.concatenate([keep2 + got2, keep3[shares[0] :]], axis=0)
    got2 = step(keep2, 0)
    pieces = [(0, unit, own_rows, None, 0), (0, unit + own_rows, own_rows, None, w1), (1, unit, unit, 0, 0), (2, 0, unit, 1, 0)]
    early = [v for pair in (first, second, third) for v in pair]
    root, off, upper = place(owners, pieces, where, early, unit, w0, w2)
    keep, got, root, off, upper = hold([], keep, got, root, off, upper)
    keep = keep + got
    got = step(keep, 1)
    keep2, got2 = hold([], keep2, got2)
    keep2 = keep2 + got2
    got2 = step(keep2, 1)
    keep, got = hold([], keep, got)
    places = (tables[3][::2], owners[2], where)
    off, upper = finish(0, *places, (keep, got), off, upper, unit, halves, shares)
    shapes = [(w1 // 2, w1), (w1, w2), (w2, w2)]
    off, upper, sep, middle, lower = finish(1, *places, (keep, got, keep2, got2), off, upper, unit, halves, shares, shapes)
    return root, off[None], sep[None], upper[None], middle[None], lower[None]


def solution(mesh):
    n_pole, n_row, n_col = (mesh.shape[axis] for axis in ("pole", "row", "col"))

    def shards(root_inverse, node_factor, *rest):
        fits = n_col == 2 and n_row == 4 and n_pole == 4
        form = functools.partial(paired, n_pole, n_row) if fits else general
        return form(root_inverse, node_factor, *rest)

    return jax.shard_map(
        shards,
        mesh=mesh,
        in_specs=(
            P("pole", ("row", "col"), None),
            P("pole", "row", None, "col"),
            P("pole", "row", None, None),
            P("pole", ("row", "col"), None, None),
            P("pole", ("row", "col"), None, None),
            P("pole", ("row", "col"), None, None),
            P(("row", "col"), None),
            P("pole"),
        ),
        out_specs=(
            P(("row", "col"), None),
            P("row", None, "col"),
            P("row", "col", None),
            P(("row", "col"), None, None),
            P(("row", "col"), None, None),
            P(("row", "col"), None, None),
        ),
        check_vma=False,
    )
```

```python
import functools

import jax
import jax.numpy as jnp
from jax import lax
from jax.experimental import pallas as pl
from jax.experimental.pallas import tpu as pltpu
from jax.sharding import PartitionSpec as P

HIGH = lax.Precision.HIGH
SWAP = [(0, 1), (1, 0)]
MIB = 1 << 20


def product(left, right):
    return jnp.matmul(left, right, precision=HIGH)


def left_t(left, right):
    return jnp.einsum("pki,pkj->pij", left, right, precision=HIGH)


def weighted(weights, values):
    return jnp.sum(weights[:, None, None] * values, axis=0)


def general(
    root_inverse,
    node_factor,
    node_inverse,
    leaf_root_factor,
    leaf_node_factor,
    leaf_inverse,
    leaf_pattern,
    pole_weight,
):
    inv_n, leaf_n, inv_l = node_inverse[:, 0], leaf_node_factor[:, 0], leaf_inverse[:, 0]
    w1, width = inv_n.shape[2], node_factor.shape[3]
    start = lax.axis_index("col") * width
    row_mask = jnp.repeat(leaf_pattern[0].astype(jnp.float32), leaf_root_factor.shape[2] // leaf_pattern.shape[1])
    leaf = leaf_root_factor[:, 0] * row_mask[None, :, None]
    factor = lax.all_gather(node_factor[:, 0], "col", axis=2, tiled=True)
    root = lax.all_gather(root_inverse, ("row", "col"), axis=1, tiled=True)
    x = product(root, jnp.concatenate([factor, leaf - product(factor, leaf_n)], axis=2))
    gram = left_t(jnp.concatenate([factor, leaf], axis=2), x)
    sep = inv_n + gram[:, :w1, :w1]
    middle = jnp.swapaxes(gram[:, w1:, :w1], 1, 2) - product(sep, leaf_n)
    lower = inv_l + gram[:, w1:, w1:] - left_t(leaf_n, middle)
    rows = -weighted(pole_weight, x)
    totals = lax.psum(
        (
            weighted(pole_weight, root_inverse),
            lax.dynamic_slice_in_dim(rows, start, width, 1),
            lax.dynamic_slice_in_dim(weighted(pole_weight, sep), start, width, 0),
            rows[:, w1:],
            weighted(pole_weight, middle),
            weighted(pole_weight, lower),
        ),
        "pole",
    )
    return (totals[0],) + tuple(t[None] for t in totals[1:])


VMEM = pl.BlockSpec(memory_space=pltpu.VMEM)
SMEM = pl.BlockSpec(memory_space=pltpu.SMEM)
ACROSS = ((0,), (0,))


def call(kernel, name, outs, args, smem, **options):
    return pl.pallas_call(
        kernel,
        in_specs=[SMEM] * smem + [VMEM] * (len(args) - smem),
        out_specs=[VMEM] * len(outs),
        out_shape=outs,
        compiler_params=pltpu.CompilerParams(vmem_limit_bytes=20 * MIB),
        cost_estimate=pl.CostEstimate(flops=1, bytes_accessed=1, transcendentals=0),
        name=name,
        **options,
    )(*args)


def split(x):
    high = x.astype(jnp.bfloat16)
    return high, (x - high.astype(jnp.float32)).astype(jnp.bfloat16)


def dot3(left, right, dims=((1,), (0,))):
    def one(a, b):
        return lax.dot_general(a, b, (dims, ((), ())), preferred_element_type=jnp.float32)

    k = dims[0][0]
    return one(
        jnp.concatenate([left[0], left[0], left[1]], axis=k), jnp.concatenate([right[0], right[1], right[0]], axis=0)
    )


def pick(table, row):
    value = jnp.int32(table[0])
    for j in range(1, len(table)):
        value = jnp.where(row == j, table[j], value)
    return value


def prepare_kernel(
    where, pattern, f_other, f_hbm, leaf_hbm, leaf_n_hbm, w_high, w_low, l_high, l_low, f_own, leaf, leaf_n, sems, n_sems
):
    poles, w0, width = f_own.shape
    w1 = 2 * width
    block = w0 // pattern.shape[1]
    rows = w0 // sems.shape[1]
    first = where[0] == 0

    def copies(p, i):
        here = pl.ds(i * rows, rows)
        return [
            pltpu.make_async_copy(hbm.at[p, here], ref.at[p, here], sems.at[p, i, j])
            for j, (hbm, ref) in enumerate([(f_hbm, f_own), (leaf_hbm, leaf)])
        ]

    def copy_n(p):
        return pltpu.make_async_copy(leaf_n_hbm.at[p], leaf_n.at[p], n_sems.at[p])

    for p in range(poles):
        copy_n(p).start()
        for i in range(w0 // rows):
            for copy in copies(p, i):
                copy.start()
    for p in range(poles):
        copy_n(p).wait()
        ns = split(leaf_n[p])
        for i in range(w0 // rows):
            for copy in copies(p, i):
                copy.wait()
            here = pl.ds(i * rows, rows)
            own, other = f_own[p, here], f_other[p, here]
            f = jnp.concatenate([jnp.where(first, own, other), jnp.where(first, other, own)], axis=1)
            masked = leaf[p, here]
            kept = []
            for j in range(0, rows, block):
                kept.append(jnp.where(pattern[0, (i * rows + j) // block] != 0, masked[j : j + block], 0.0))
            masked = jnp.concatenate(kept, axis=0)
            fs = split(f)
            ds = split(masked - dot3(fs, ns))
            w_high[p, here, :w1], w_low[p, here, :w1] = fs
            w_high[p, here, w1:], w_low[p, here, w1:] = ds
            l_high[p, here], l_low[p, here] = split(masked)


def prepare(where, pattern, f_own, f_other, leaf, leaf_n):
    poles, w0, width = f_own.shape
    w1, w2 = leaf_n.shape[1:]
    parts = 4
    hbm = [pltpu.with_memory_space_constraint(x, pltpu.HBM) for x in (f_own, leaf, leaf_n)]
    return pl.pallas_call(
        prepare_kernel,
        in_specs=[SMEM] * 2 + [VMEM] + [pl.BlockSpec(memory_space=pltpu.HBM)] * 3,
        out_specs=[VMEM] * 4,
        out_shape=[pltpu.VMEM((poles, w0, n), jnp.bfloat16) for n in (w1 + w2, w1 + w2, w2, w2)],
        scratch_shapes=[
            pltpu.VMEM((poles, w0, width), jnp.float32),
            pltpu.VMEM((poles, w0, w2), jnp.float32),
            pltpu.VMEM((poles, w1, w2), jnp.float32),
            pltpu.SemaphoreType.DMA((poles, parts, 2)),
            pltpu.SemaphoreType.DMA((poles,)),
        ],
        compiler_params=pltpu.CompilerParams(vmem_limit_bytes=20 * MIB),
        cost_estimate=pl.CostEstimate(flops=1, bytes_accessed=1, transcendentals=0),
        name="prepare",
    )(where, pattern, f_other, *hbm)


def unit_kernel(form, slots, cuts, owners, slot_of, ways, where, weight, *refs):
    count = {"first": 1, "next": 2, "halves": 2, "part": 1, "last": 1}[form]
    shards = []
    for n in cuts:
        shards.append(refs[:n])
        refs = refs[n:]
    (w_high, w_low, l_high, l_low), refs = refs[:4], refs[4:]
    if form in ("next", "halves", "last"):
        (gram_in, square_in), refs = refs[:2], refs[2:]
    if form == "last":
        (kept_high, kept_low, inv_n), refs = refs[:3], refs[3:]
    if form == "last":
        outs, (r_high, r_low, sent_at, sep_at) = refs[:-4], refs[-4:]
    else:
        outs, (r_high, r_low) = refs[:-2], refs[-2:]
    col, row = where[0], where[1]
    owner, slot, way = (pick(table, row) for table in (owners, slot_of, ways))
    poles, rows, _ = shards[0][0].shape
    w2 = l_high.shape[2]
    w1 = w_high.shape[2] - w2
    width = w1 // 2
    begin = [pl.multiple_of(jnp.where(way == i, 0, rows), rows) for i in range(2)]
    if form == "first":
        for i in range(2):
            at = pl.ds(pl.multiple_of(jnp.where(col == i, 0, rows), rows), rows)
            for p in range(poles):
                r_high[p, at], r_low[p, at] = split(shards[i][0][p])
    else:
        for i in range(count):
            at = pl.ds(begin[i] if count == 2 else 0, rows)
            for s in range(slots):
                for j in range(2):
                    pieces = shards[(2 * s + j) * count + i]

                    @pl.when((slot == s) & ((way == col) == (j == 0)))
                    def _():
                        for p in range(poles):
                            piece = pieces[p * len(pieces) // poles]
                            r_high[p, at], r_low[p, at] = split(piece[p % piece.shape[0]])

    span = r_high.shape[1]
    base = owner * 2 * rows
    if form == "last":
        heres = [pl.ds(pl.multiple_of(base + begin[i], rows), rows) for i in range(2)]
    else:
        heres = [pl.ds(pl.multiple_of(base, 2 * rows), span)]
    for p in range(poles):
        x = dot3((r_high[p], r_low[p]), (w_high[p], w_low[p]))
        scale = weight[p]
        mine = jnp.where(col == 0, x[:, :width], x[:, width:w1])
        sent = -scale * jnp.concatenate([mine, x[:, w1:]], axis=1)
        sent_ref = sent_at if form == "last" else outs[0]
        if form in ("halves", "part"):
            total = sent if p == 0 else total + sent
        elif p == 0:
            sent_ref[...] = sent
        else:
            sent_ref[...] += sent
        xs = split(x)
        if form == "part":
            outs[2][p], outs[3][p] = xs
            continue
        if form == "last":
            xs = [jnp.concatenate([kept[p], v], axis=0) for kept, v in zip((kept_high, kept_low), xs)]
        fs = [jnp.concatenate([w[p, here, :w1] for here in heres], axis=0) for w in (w_high, w_low)]
        ls = [jnp.concatenate([l[p, here] for here in heres], axis=0) for l in (l_high, l_low)]
        ps = [v[:, :w1] for v in xs]
        us = [v[:, w1:] for v in xs]
        cross = dot3(fs, ps, ACROSS)
        below = dot3(ls, ps, ACROSS)
        inner = dot3(ls, us, ACROSS)
        if form != "first":
            cross = cross + gram_in[p, :w1]
            below = below + gram_in[p, w1:]
            inner = inner + square_in[p]
        gram, square = outs[-2:]
        gram[p, :w1] = cross
        gram[p, w1:] = below
        square[p] = inner
        if form == "last":
            sep = inv_n[p] + cross
            sep = scale * jnp.where(col == 0, sep[:width], sep[width:])
            if p == 0:
                sep_at[...] = sep
            else:
                sep_at[...] += sep
    if form in ("halves", "part"):
        for i in range(2):

            @pl.when(where[2] == i)
            def _():
                outs[i][...] = total[: span // 2]
                outs[1 - i][...] = total[span // 2 :]

    if form == "last":
        head = outs[0].shape[0] - rows
        for i in range(2):

            @pl.when(where[2] == i)
            def _():
                outs[i][:rows] = sent_at[...]
                outs[i][rows:] = sep_at[:head]
                outs[1 - i][...] = sep_at[head:]


def ends_kernel(where, weight, gram, square, inv_n, leaf_n, inv_l, keep, send, rest_at):
    poles, w1, w2 = leaf_n.shape
    width = w1 // 2
    for p in range(poles):
        ns = split(leaf_n[p])
        middle = gram[p, w1:].T - dot3(split(inv_n[p] + gram[p, :w1]), ns)
        lower = inv_l[p] + square[p] - dot3(ns, split(middle), ACROSS)
        middle = jnp.concatenate([middle[:width], middle[width:]], axis=1)
        lower = jnp.concatenate([lower[: w2 // 2], lower[w2 // 2 :]], axis=1)
        value = weight[p] * jnp.concatenate([middle, lower], axis=0)
        if p == 0:
            rest_at[...] = value
        else:
            rest_at[...] += value
    head = keep.shape[0]
    for i, (a, b) in enumerate([(keep, send), (send, keep)]):

        @pl.when(where[2] == i)
        def _():
            a[...] = rest_at[:head]
            b[...] = rest_at[head:]


def ends_call(where, weight, gram, square, inv_n, leaf_n, inv_l):
    w1, w2 = leaf_n.shape[1:]
    rows = (w1 + w2) // 2
    outs = [pltpu.VMEM((rows // 2, w1), jnp.float32)] * 2
    args = [where, weight, gram, square, inv_n, leaf_n, inv_l]
    return call(ends_kernel, "ends", outs, args, 2, scratch_shapes=[pltpu.VMEM((rows, w1), jnp.float32)])


def unit_call(form, tables, where, weight, shards, factors, sums=(), ends=()):
    poles, rows, w0 = shards[0][0].shape
    lanes, w2 = factors[0].shape[2], factors[2].shape[2]
    w1 = lanes - w2
    f32 = jnp.float32
    gram = [pltpu.VMEM((poles, lanes, w1), f32), pltpu.VMEM((poles, w2, w2), f32)]
    outs = {
        "first": [pltpu.VMEM((2 * rows, w1), f32)] + gram,
        "next": [pltpu.VMEM((2 * rows, w1), f32)] + gram,
        "halves": [pltpu.VMEM((rows, w1), f32)] * 2 + gram,
        "part": [pltpu.VMEM((rows // 2, w1), f32)] * 2 + [pltpu.VMEM((poles, rows, lanes), jnp.bfloat16)] * 2,
        "last": [pltpu.VMEM(((rows + w1 // 2) // 2, w1), f32)] * 2 + gram,
    }[form]
    cuts = [len(pieces) for pieces in shards]
    args = [where, weight, *(x for pieces in shards for x in pieces), *factors, *sums, *ends]
    slots = len(shards) // (4 if form in ("next", "halves") else 2)
    span = rows * (1 if form in ("part", "last") else 2)
    options = {"scratch_shapes": [pltpu.VMEM((poles, span, w0), jnp.bfloat16)] * 2}
    if form == "last":
        options["scratch_shapes"] += [pltpu.VMEM((rows, w1), f32), pltpu.VMEM((w1 // 2, w1), f32)]
        at = len(args) - len(ends) - 2
        options["input_output_aliases"] = {at: 2, at + 1: 3}
    if form in ("next", "halves"):
        at = 2 if form == "halves" else 1
        options["input_output_aliases"] = {len(args) - 2: at, len(args) - 1: at + 1}
    return list(call(functools.partial(unit_kernel, form, slots, cuts, *tables), form, outs, args, 2, **options))


def place_kernel(unit, owners, pieces, where, *refs):
    sums, (root, off, upper) = refs[:-3], refs[-3:]
    width = off.shape[1]
    for pair, start, rows, k, at in pieces:
        here = pl.ds(start, rows)
        total = sums[2 * pair][here] + sums[2 * pair + 1][here]
        if k is None:
            root[:, at : at + total.shape[1]] = total
            continue
        there = pl.ds(pl.multiple_of(pick(owners[k], where[1]) * unit + at, unit // 2), rows)
        off[there] = total[:, :width]
        upper[there] = total[:, width:]


def place(owners, pieces, where, sums, unit, w0, w2):
    w1 = sums[0].shape[1]
    outs = [jax.ShapeDtypeStruct(o, jnp.float32) for o in [(unit // 2, w0), (w0, w1 // 2), (w0, w2)]]
    return call(functools.partial(place_kernel, unit, owners, pieces), "place", outs, [where, *sums], 1)


def send_out(copies, sem):
    copies = [pltpu.make_async_copy(a, b, sem.at[i]) for i, (a, b) in enumerate(copies)]
    for copy in copies:
        copy.start()
    for copy in copies:
        copy.wait()


def rows_kernel(unit, table, owners, where, kept, got, _off, _upper, off, upper, sep, sem):
    rows = unit // 2
    width = off.shape[1]
    base, way = (pick(t, where[1]) for t in table)
    last, before = base * unit, pick(owners, where[1]) * unit
    second_at = last + jnp.where(way == 1, 0, rows)
    head = kept.shape[0] - rows
    for i, halves in enumerate([(kept, got), (got, kept)]):

        @pl.when(where[2] == i)
        def _():
            moves = [(halves[0], 0, rows, second_at)]
            for j, half in enumerate(halves):
                moves.append((half, head, rows, before + j * rows))
            copies = []
            for half, start, size, place in moves:
                there = pl.ds(pl.multiple_of(place, rows), size)
                for k, out in enumerate([off, upper]):
                    copies.append((half.at[pl.ds(start, size), pl.ds(k * width, width)], out.at[there]))
            rest = head - rows
            copies.append((halves[0].at[pl.ds(rows, rest)], sep.at[pl.ds(0, rest)]))
            copies.append((halves[1].at[pl.ds(0, head)], sep.at[pl.ds(rest, head)]))
            send_out(copies, sem)


def leaf_kernel(unit, table, flip, where, half, *refs):
    off, upper, middle, lower, sem = refs[-5:]
    w1, w2 = middle.shape
    width, rows = w1 // 2, unit // 4
    size = half.shape[0] - rows
    rest = width - size
    base, way = (pick(t, where[1]) for t in table)
    index = where[2] if flip == 0 else 1 - where[2]
    there = base * unit + jnp.where(way == 0, 0, 2 * rows) + index * rows
    there = pl.ds(pl.multiple_of(there, rows), rows)

    def lanes(start, n, k):
        return half.at[pl.ds(start, n), pl.ds(k * w2, w2)]

    shared = [
        (half.at[pl.ds(size, rows), pl.ds(k * out.shape[1], out.shape[1])], out.at[there])
        for k, out in enumerate([off, upper])
    ]

    @pl.when(index == 0)
    def _():
        send_out(shared + [(lanes(0, size, k), middle.at[pl.ds(k * width, size)]) for k in range(2)], sem)

    @pl.when(index == 1)
    def _():
        copies = [(lanes(0, rest, k), middle.at[pl.ds(k * width + size, rest)]) for k in range(2)]
        n = w2 // 2
        copies += [(lanes(rest, n, k), lower.at[pl.ds(k * n, n)]) for k in range(2)]
        send_out(shared + copies, sem)


def place_out(kernel, name, where, sums, into, shapes, copies):
    anywhere = pl.BlockSpec(memory_space=pl.ANY)
    return pl.pallas_call(
        kernel,
        in_specs=[SMEM] + [VMEM] * len(sums) + [anywhere] * len(into),
        out_specs=[anywhere] * (len(into) + len(shapes)),
        out_shape=[jax.ShapeDtypeStruct(s, jnp.float32) for s in [x.shape for x in into] + list(shapes)],
        scratch_shapes=[pltpu.SemaphoreType.DMA((copies,))],
        input_output_aliases={1 + len(sums) + i: i for i in range(len(into))},
        compiler_params=pltpu.CompilerParams(vmem_limit_bytes=20 * MIB),
        cost_estimate=pl.CostEstimate(flops=1, bytes_accessed=1, transcendentals=0),
        name=name,
    )(where, *sums, *into)


def line_plan(n):
    plan = []
    for j in range(n):
        above = [(s, 0, j + s) for s in range(1, n - j)]
        below = [(s, 1, j - s) for s in range(1, j + 1)]
        plan.append(sorted(above + below, key=lambda e: (e[0], e[1] if j < n // 2 else -e[1])))
    return plan


def together(*groups):
    flat, tree = jax.tree.flatten(groups)
    return jax.tree.unflatten(tree, lax.optimization_barrier(tuple(flat)))


def paired(
    n_pole,
    n_row,
    root_inverse,
    node_factor,
    node_inverse,
    leaf_root_factor,
    leaf_node_factor,
    leaf_inverse,
    leaf_pattern,
    pole_weight,
):
    pole, col = lax.axis_index("pole"), lax.axis_index("col")
    far = jnp.where(col == 0, pole // 2, pole & 1)
    where = jnp.stack([col, lax.axis_index("row"), far]).astype(jnp.int32)
    w0 = root_inverse.shape[2]
    w1, w2 = leaf_node_factor.shape[2:]
    own_rows = root_inverse.shape[1]
    unit = 2 * own_rows
    units = [[(0, 0, j) for j in range(n_row)]] + [list(unit) for unit in zip(*line_plan(n_row))]
    slots = [sorted({e[0] for e in unit}) for unit in units]
    tables = [
        ([e[2] for e in unit], [slot.index(e[0]) for e in unit], [e[1] for e in unit]) for unit, slot in zip(units, slots)
    ]
    owners = [table[0] for table in tables]
    moved, other = {}, {}

    def advance(slot, i):
        down = [(2 * j, 2 * (j - 1)) for j in range(1, n_row - slot + 1)]
        up = [(2 * j + 1, 2 * j + 3) for j in range(slot - 1, n_row - 1)]
        moved[slot, i] = lax.ppermute(moved[slot - 1, i], ("row", "col"), down + up)

    def swap(key, cuts=1):
        size = moved[key].shape[0] // cuts
        pieces = [moved[key][i * size : (i + 1) * size] for i in range(cuts)] if cuts > 1 else [moved[key]]
        other[key] = tuple(lax.ppermute(piece, "col", SWAP) for piece in pieces)

    token = pole_weight

    def hold(keys, *rest):
        nonlocal token
        got, over, token, rest = together(
            [moved[key] for key in keys], [other[key] for key in keys if key in other], token, rest
        )
        moved.update(zip(keys, got, strict=True))
        other.update(zip([key for key in keys if key in other], over, strict=True))
        return rest

    def step(value, turn):
        pairs = [(2 * p + c, 2 * (p ^ (1 << (c ^ turn))) + c) for p in range(n_pole) for c in range(2)]
        return lax.ppermute(value, ("pole", "col"), pairs)

    def cut(pair, rows):
        return pair[0][:rows] + pair[1][:rows]

    def unit_of(form, k, which, *rest):
        shards = []
        for slot in slots[k]:
            shards += [(moved[slot, i],) for i in which] + [other[slot, i] for i in which]
        return unit_call(form, tables[k], where, token, shards, *rest)

    f_own = node_factor[:, 0]
    f_other = lax.ppermute(f_own, "col", SWAP)
    moved[0, 0] = root_inverse
    advance(1, 0)
    swap((0, 0))
    (moved[0, 1],) = other[0, 0]
    advance(1, 1)
    factors = prepare(where, leaf_pattern, f_own, f_other, leaf_root_factor[:, 0], leaf_node_factor[:, 0])
    factors, root = together(factors, root_inverse)
    root = weighted(pole_weight, root)
    root = jnp.concatenate([root[:, :w1], root[:, w1:]], axis=0)
    roots = (root, step(root, 0))

    (factors,) = hold([(1, 0)], factors)
    swap((1, 0))
    advance(2, 0)
    rows, *sums = unit_of("first", 0, (0,), factors)
    rows, sums = hold([(1, 1)], rows, sums)
    (roots,) = hold([], roots)
    value = jnp.concatenate([rows, roots[0] + roots[1]], axis=0)
    first = (value, step(value, 1))
    swap((1, 1))
    advance(2, 1)
    hold([(1, 0)])

    hold([(2, 0)])
    swap((2, 0))
    advance(3, 0)
    (first,) = hold([], first)
    value = cut(first, unit)
    second = (value, step(value, 0))
    hold([(1, 1)])
    rows, *sums = unit_of("next", 1, (0, 1), factors, sums)
    rows, sums, second = hold([], rows, sums, second)
    rows, sums = hold([(2, 1)], rows, sums)
    swap((2, 1))
    third = (rows, step(rows, 1))
    advance(3, 1)
    hold([(2, 0)])

    hold([(3, 0)])
    swap((3, 0), 2)
    (third,) = hold([], third)
    value = third[0] + third[1]
    fourth = (value, step(value, 0))
    hold([(2, 1)])
    keep3, send3, *sums = unit_of("halves", 2, (0, 1), factors, sums)
    keep3, send3, sums, fourth = hold([], keep3, send3, sums, fourth)

    hold([(3, 0)])
    kept = unit_of("part", 3, (0,), factors)
    kept, keep3, send3 = hold([(3, 1)], kept, keep3, send3)
    swap((3, 1))
    keep4, send4, *kept = kept
    got3 = step(jnp.concatenate([send3, send4], axis=0), 1)
    hold([(3, 1)])
    inv_n = node_inverse[:, 0]
    keep, send, *sums = unit_of("last", 3, (1,), factors, sums, (*kept, inv_n))
    keep, send, sums, (keep3, keep4), got3 = hold([], keep, send, sums, (keep3, keep4), got3)
    got = step(send, 1)
    keep2, send2 = ends_call(where, token, *sums, inv_n, leaf_node_factor[:, 0], leaf_inverse[:, 0])
    keep2, send2 = hold([], keep2, send2)
    got2 = step(send2, 1)
    keep3 = keep3 + got3[:own_rows]
    keep, got = hold([], keep, got)
    keep = jnp.concatenate([keep + got, keep3], axis=0)
    got = step(keep, 0)
    keep2, got2 = hold([], keep2, got2)
    keep2 = jnp.concatenate([keep2 + got2, keep4 + got3[own_rows:]], axis=0)
    got2 = step(keep2, 0)
    pieces = [(0, unit, own_rows, None, 0), (0, unit + own_rows, own_rows, None, w1), (1, 0, unit, 0, 0), (2, 0, unit, 1, 0)]
    early = [v for pair in (first, second, fourth) for v in pair]
    root, off, upper = place(owners, pieces, where, early, unit, w0, w2)
    keep, got, root, off, upper = hold([], keep, got, root, off, upper)
    keep = keep + got
    got = step(keep, 1)
    keep2, got2 = hold([], keep2, got2)
    keep2 = keep2 + got2
    got2 = step(keep2, 1)
    (keep2,) = hold([], keep2)
    blocks = [(w1, w2), (w2, w2)]
    kernels = [functools.partial(leaf_kernel, unit, tables[3][::2], flip) for flip in range(2)]
    off, upper, middle, lower = place_out(kernels[0], "leaf", where, [keep2], [off, upper], blocks, 6)
    keep, got, off, upper, middle, lower = hold([], keep, got, off, upper, middle, lower)
    kernel = functools.partial(rows_kernel, unit, tables[3][::2], owners[2])
    off, upper, sep = place_out(kernel, "rows", where, [keep, got], [off, upper], [(w1 // 2, w1)], 8)
    off, upper, sep, got2 = hold([], off, upper, sep, got2)
    off, upper, middle, lower = place_out(kernels[1], "leaf", where, [got2], [off, upper, middle, lower], [], 6)
    return root, off[None], sep[None], upper[None], middle[None], lower[None]


def solution(mesh):
    n_pole, n_row, n_col = (mesh.shape[axis] for axis in ("pole", "row", "col"))

    def shards(root_inverse, node_factor, *rest):
        fits = n_col == 2 and n_row == 4 and n_pole == 4
        form = functools.partial(paired, n_pole, n_row) if fits else general
        return form(root_inverse, node_factor, *rest)

    return jax.shard_map(
        shards,
        mesh=mesh,
        in_specs=(
            P("pole", ("row", "col"), None),
            P("pole", "row", None, "col"),
            P("pole", "row", None, None),
            P("pole", ("row", "col"), None, None),
            P("pole", ("row", "col"), None, None),
            P("pole", ("row", "col"), None, None),
            P(("row", "col"), None),
            P("pole"),
        ),
        out_specs=(
            P(("row", "col"), None),
            P("row", None, "col"),
            P("row", "col", None),
            P(("row", "col"), None, None),
            P(("row", "col"), None, None),
            P(("row", "col"), None, None),
        ),
        check_vma=False,
    )
```
